512 devices in a mesh: dp: 16 (over x, z_hi), row: 4 (over z_lo), col: 8 (over y, core).
Axes of the slice: x: 4, y: 4, z: 16 (z_hi: 4, z_lo: 4; z = z_hi * 4 + z_lo), core: 2. Of those that a mesh axis runs over, the one named last changes fastest.
Arguments:
- queries: bfloat16 [16, 48, 128, 1024], P('dp', 'row', 'col'), may hold values from -6 to 6
- keyvals: bfloat16 [16, 2, 48, 128, 1024], P('dp', None, 'row', 'col'), may hold values from -6 to 6
- out_weight: bfloat16 [16, 1024, 2048], P('dp', ('row', 'col')), may hold values from -0.75 to 0.75
- gate_weight: bfloat16 [16, 2048, 2048], P('dp', ('row', 'col')), may hold values from -0.125 to 0.125
- class_table: bfloat16 [16, 1000, 2048], P('dp', None, ('row', 'col')), may hold values from -5 to 5
- labels: int32 [16], P('dp'), may hold values from 0 to 999
- timesteps: int32 [16], P('dp'), may hold values from 0 to 999
- round_index: int32 [1], replicated, may hold values from 0 to 996
Outputs:
- update: bfloat16 [16, 48, 128, 2048], P('dp', 'row', 'col')
The draws below stay inside these ranges and needn't reach their ends.
All inputs are finite; a program needn't handle non-finite values.
Results may differ from the reference program's by a relative error of at most 0.0081.
Values may be sent and summed in bfloat16 or wider, within the bound.
No kernel may reach another device: no remote copies, remote signals or barrier semaphores. Data moves between devices by JAX's collectives and lax.ppermute only.
A program may use at most 64 MiB of HBM per device.

```python
import math
import jax
import jax.numpy as jnp
from jax import lax

D = 2048
HEADS = 8
HDIM = 128
CLASSES = 1000
RADIUS = 3
INNER = 1024
IMAGES = 16
GRID_ROWS = 48
GRID_COLS = 128
N_DP = 16


def draw_queries(key, part):
    key = jax.random.fold_in(key, 11)
    shape_all = (IMAGES, GRID_ROWS, GRID_COLS, INNER)
    base_draw = jnp.clip(jax.random.normal(key, shape_all, jnp.float32), -4.0, 4.0)
    return base_draw.astype(jnp.bfloat16)


def draw_keyvals(key, part):
    key = jax.random.fold_in(key, 12)
    shape_all = (IMAGES, 2, GRID_ROWS, GRID_COLS, INNER)
    base_draw = jnp.clip(jax.random.normal(key, shape_all, jnp.float32), -4.0, 4.0)
    return base_draw.astype(jnp.bfloat16)


def plant(array, rng, least, largest):
    extent = array.shape
    spot = [jax.random.randint(jax.random.fold_in(rng, axis), (), 0, extent[axis]) for axis in range(len(extent))]
    array = array.at[tuple(spot)].set(least)
    longest = extent.index(max(extent))
    spot[longest] = (spot[longest] + 1) % extent[longest]
    return array.at[tuple(spot)].set(largest)


def block_levels(stream_key, dims, pieces, smallest, largest):
    def one(dim, blocks):
        draws = jax.random.uniform(jax.random.fold_in(jax.random.fold_in(stream_key, 6), dim), (blocks,), jnp.float32, smallest / len(pieces), largest / len(pieces))
        return jnp.repeat(jnp.exp(draws), dims[dim] // blocks).reshape((-1,) + (1,) * (len(dims) - dim - 1))

    factor_of = one(*pieces[0])
    for cut in pieces[1:]:
        factor_of = factor_of * one(*cut)
    return factor_of


def centred(rng, dims, scale, most, pieces=(), kind=jnp.bfloat16):
    array = scale * jax.random.normal(rng, dims, jnp.float32)
    if pieces:
        array = array * block_levels(rng, dims, pieces, -0.22, 0.18)
    return jnp.clip(array, -most, most).astype(kind)


def setup_inputs(seed: int = 0) -> dict:
    key_of = jax.random.split(jax.random.key(seed), 9)
    queries = draw_queries(jax.random.fold_in(key_of[8], 71), 0)
    keyvals = draw_keyvals(jax.random.fold_in(key_of[8], 71), 0)
    out_weight = centred(key_of[2], (IMAGES, INNER, D), (INNER // 16) ** -0.5, 0.75, ((0, 16), (1, 32)))
    gate_weight = centred(key_of[3], (IMAGES, D, D), D ** -0.5, 0.125, ((0, 16), (1, 32)))
    class_table = centred(key_of[4], (IMAGES, CLASSES, D), 1.0, 5.0, ((0, 16), (2, 32)))
    labels = plant(jax.random.randint(key_of[5], (IMAGES,), 0, CLASSES), jax.random.fold_in(key_of[5], 1), 0, CLASSES - 1).astype(jnp.int32)
    timesteps = plant(jax.random.randint(key_of[6], (IMAGES,), 0, 1000), jax.random.fold_in(key_of[6], 1), 0, 999).astype(jnp.int32)
    round_index = jax.random.randint(key_of[7], (1,), 0, 997).astype(jnp.int32)
    return dict(queries=queries, keyvals=keyvals, out_weight=out_weight, gate_weight=gate_weight, class_table=class_table, labels=labels, timesteps=timesteps, round_index=round_index)


def time_embed(step_value, width):
    half_width = width // 2
    positions = jnp.arange(width)
    freq_index = (positions % half_width).astype(jnp.float32)
    frequency = jnp.exp(-math.log(10000.0) * freq_index / half_width)
    angle_value = step_value * frequency
    return jnp.where(positions < half_width, jnp.cos(angle_value), jnp.sin(angle_value))

def mix_params(params, distance):
    shifted = jnp.roll(params, distance, axis=0)
    return (0.5 * (params.astype(jnp.float32) + shifted.astype(jnp.float32))).astype(jnp.bfloat16)

def attend(query_img, keyval_img):
    rows_total = query_img.shape[0]
    cols_total = query_img.shape[1]
    window = 2 * RADIUS + 1
    score_scale = 1.0 / math.sqrt(HDIM)
    query_heads = query_img.reshape(rows_total, cols_total, HEADS, HDIM).astype(jnp.float32)
    padded = jnp.pad(keyval_img, ((0, 0), (RADIUS, RADIUS), (RADIUS, RADIUS), (0, 0)))
    padded = padded.reshape(2, rows_total + 2 * RADIUS, cols_total + 2 * RADIUS, HEADS, HDIM)
    inside = jnp.pad(jnp.ones((rows_total, cols_total), jnp.bool_), RADIUS)
    score_list = []
    for row_off in range(window):
        for col_off in range(window):
            key_here = padded[0, row_off:row_off + rows_total, col_off:col_off + cols_total].astype(jnp.float32)
            score_here = jnp.einsum('xyhd,xyhd->xyh', query_heads, key_here) * score_scale
            valid = inside[row_off:row_off + rows_total, col_off:col_off + cols_total]
            score_list.append(jnp.where(valid[:, :, None], score_here, jnp.float32(-1e+30)))
    scores = jnp.stack(score_list, axis=-1)
    row_max = lax.optimization_barrier(jnp.max(scores, axis=-1, keepdims=True))
    exponent = jnp.exp(scores - row_max)
    probs = (exponent / lax.optimization_barrier(jnp.sum(exponent, axis=-1, keepdims=True))).astype(jnp.bfloat16)
    attended = jnp.zeros((rows_total, cols_total, HEADS, HDIM), jnp.float32)
    for row_off in range(window):
        for col_off in range(window):
            value_here = padded[1, row_off:row_off + rows_total, col_off:col_off + cols_total].astype(jnp.float32)
            weight_here = probs[..., row_off * window + col_off].astype(jnp.float32)
            attended = attended + weight_here[..., None] * value_here
    return attended.astype(jnp.bfloat16).reshape(rows_total * cols_total, HEADS * HDIM)

def reference(queries, keyvals, out_weight, gate_weight, class_table, labels, timesteps, round_index):
    bit_count = int(N_DP).bit_length() - 1
    distance = jnp.left_shift(jnp.int32(1), (round_index[0] % bit_count).astype(jnp.int32))
    out_mixed = mix_params(out_weight, distance)
    gate_mixed = mix_params(gate_weight, distance)
    table_mixed = mix_params(class_table, distance)

    def one_image(bundle):
        query_img, keyval_img, out_img, gate_img, table_img, label_img, step_img = bundle
        class_row = lax.dynamic_index_in_dim(table_img, label_img.astype(jnp.int32), 0, keepdims=False)
        embed = time_embed(step_img.astype(jnp.float32), D)
        cond = jax.nn.silu(class_row.astype(jnp.float32) + embed).astype(jnp.bfloat16)
        gate = jnp.dot(cond[None, :], gate_img, preferred_element_type=jnp.float32)[0]
        attended = attend(query_img, keyval_img)
        projected = jnp.dot(attended, out_img, preferred_element_type=jnp.float32)
        result = (gate[None, :] * projected).astype(jnp.bfloat16)
        return result.reshape(query_img.shape[0], query_img.shape[1], D)
    return lax.map(one_image, (queries, keyvals, out_mixed, gate_mixed, table_mixed, labels, timesteps))
```

```python
import math

import jax
import jax.numpy as jnp
from jax import lax
from jax.experimental import pallas as pl
from jax.experimental.pallas import tpu as pltpu
from jax.sharding import PartitionSpec as P

HDIM = 128
RADIUS = 3
F32 = jnp.float32
BF16 = jnp.bfloat16
GROUP = 4
EDGE = 4
PAD_ROWS = 2


def attend_kernel(q_ref, kv_ref, up_ref, down_ref, near_ref, far_ref, out_ref):
    rows, cols = 12, 16
    inner = q_ref.shape[1]
    row0 = lax.axis_index("row") * rows
    col_index = lax.axis_index("col")
    col0 = col_index * cols
    core = lax.rem(col_index, 2)
    near_base = jnp.where(core == 0, cols, -EDGE)
    far_base = jnp.where(core == 0, -EDGE, cols)
    queries = GROUP * cols
    band = (GROUP + 2 * RADIUS) * cols
    side = (GROUP + 2 * RADIUS + PAD_ROWS) * EDGE
    keys = band + 2 * side
    halo = RADIUS * cols
    factor = math.log2(math.e) / math.sqrt(HDIM)
    q_id = lax.broadcasted_iota(jnp.int32, (queries, keys), 0)
    k_id = lax.broadcasted_iota(jnp.int32, (queries, keys), 1)
    q_row, q_col = q_id // cols, q_id % cols
    side_id = jnp.where(k_id < band + side, k_id - band, k_id - band - side)
    k_row = jnp.where(k_id < band, k_id // cols, side_id // EDGE)
    base = jnp.where(k_id < band + side, near_base, far_base)
    k_col = jnp.where(k_id < band, k_id % cols, base + side_id % EDGE)
    d_row, d_col = k_row - q_row, k_col - q_col
    reach = (d_row >= 0) & (d_row <= 2 * RADIUS) & (d_col >= -RADIUS) & (d_col <= RADIUS)
    k_gcol = col0 + k_col
    reach = reach & (k_gcol >= 0) & (k_gcol < cols * lax.axis_size("col"))
    ones = jnp.ones((keys, HDIM), BF16)
    for group in range(rows // GROUP):
        k_grow = row0 + GROUP * group - RADIUS + k_row
        allowed = reach & (k_grow >= 0) & (k_grow < rows * lax.axis_size("row"))
        bias = jnp.where(allowed, F32(0.0), F32(-1e30))
        first = (GROUP * group - RADIUS) * cols
        last = first + band
        for head in range(inner // HDIM):
            lanes = slice(head * HDIM, (head + 1) * HDIM)

            def gathered(which):
                parts = []
                if first < 0:
                    parts.append(up_ref[which, halo + first : halo, lanes])
                parts.append(kv_ref[which, max(first, 0) : min(last, rows * cols), lanes])
                if last > rows * cols:
                    parts.append(down_ref[which, 0 : last - rows * cols, lanes])
                span = slice(GROUP * group * EDGE, GROUP * group * EDGE + side)
                parts.append(near_ref[which, span, lanes])
                parts.append(far_ref[which, span, lanes])
                return jnp.concatenate(parts, axis=0)

            q = q_ref[group * queries : (group + 1) * queries, lanes]
            scores = lax.dot_general(
                q, gathered(0), (((1,), (1,)), ((), ())), preferred_element_type=F32
            )
            scores = scores + bias
            top = jnp.max(scores, axis=-1, keepdims=True)
            weight = jnp.exp2((scores - top) * factor).astype(BF16)
            values = jnp.concatenate([gathered(1), ones], axis=1)
            both = jnp.dot(weight, values, preferred_element_type=F32)
            out_ref[group * queries : (group + 1) * queries, lanes] = (
                both[:, :HDIM] / both[:, HDIM:]
            ).astype(BF16)


def attend(q, kv, up, down, near, far):
    tokens, inner = q.shape
    return pl.pallas_call(
        attend_kernel,
        out_shape=jax.ShapeDtypeStruct((tokens, inner), BF16),
        in_specs=[pl.BlockSpec(memory_space=pltpu.VMEM)] * 6,
        out_specs=pl.BlockSpec(memory_space=pltpu.VMEM),
        compiler_params=pltpu.CompilerParams(vmem_limit_bytes=20 * 2**20),
        cost_estimate=pl.CostEstimate(flops=1_200_000_000, bytes_accessed=3_000_000, transcendentals=400_000),
        name="attend",
    )(q, kv, up, down, near, far)


def project_kernel(a_ref, gate_ref, *refs):
    pieces, (out_ref, w_ref, sems) = refs[:8], refs[8:]
    row, col = lax.axis_index("row"), lax.axis_index("col")
    core, place = lax.rem(col, 2), lax.div(col, 2)
    shard = 32
    copies = []
    for plane in range(2):
        owner_core = core if plane == 0 else 1 - core
        for step in range(4):
            owner_place = lax.rem(place + 4 - step, 4)
            for back in range(4):
                owner_row = lax.rem(row + 4 - back, 4)
                start = ((owner_row * 4 + owner_place) * 2 + owner_core) * shard
                copy = pltpu.make_async_copy(
                    pieces[plane * 4 + step].at[pl.ds(back * shard, shard), :],
                    w_ref.at[pl.ds(pl.multiple_of(start, shard), shard), :],
                    sems.at[(plane * 4 + step) * 4 + back],
                )
                copy.start()
                copies.append(copy)
    for copy in copies:
        copy.wait()
    width = 512
    for part in range(out_ref.shape[1] // width):
        lanes = slice(part * width, (part + 1) * width)
        total = jnp.dot(a_ref[...], w_ref[:, lanes], preferred_element_type=F32)
        out_ref[:, lanes] = (gate_ref[:, lanes] * total).astype(BF16)


def project(a, gate, pieces):
    tokens, inner = a.shape
    width = gate.shape[1]
    return pl.pallas_call(
        project_kernel,
        out_shape=jax.ShapeDtypeStruct((tokens, width), BF16),
        in_specs=[pl.BlockSpec(memory_space=pltpu.VMEM)] * 2 + [pl.BlockSpec(memory_space=pl.ANY)] * 8,
        out_specs=pl.BlockSpec(memory_space=pltpu.VMEM),
        scratch_shapes=[pltpu.VMEM((inner, width), BF16), pltpu.SemaphoreType.DMA((32,))],
        compiler_params=pltpu.CompilerParams(vmem_limit_bytes=24 * 2**20),
        cost_estimate=pl.CostEstimate(flops=810_000_000, bytes_accessed=6_000_000, transcendentals=0),
        name="project",
    )(a, gate, *pieces)


def two_rows(value):
    high = lax.reduce_precision(value, 8, 7)
    return jnp.stack([high, value - high]).astype(BF16)


def summed(rows):
    return rows[0].astype(F32) + rows[1].astype(F32)


def cond_shard(row_a, row_b, step, positions, half_width):
    mixed = lax.reduce_precision(0.5 * (row_a + row_b), 8, 7)
    freq_index = (positions % half_width).astype(F32)
    frequency = jnp.exp(-math.log(10000.0) * freq_index / half_width)
    angle = step * frequency
    embed = jnp.where(positions < half_width, jnp.cos(angle), jnp.sin(angle))
    return jax.nn.silu(mixed + embed).astype(BF16)


def body(distance, queries, keyvals, out_weight, gate_weight, class_table, label, step):
    dp_count, row_count, col_count = (lax.axis_size(a) for a in ("dp", "row", "col"))
    ahead = [(i, (i + distance) % dp_count) for i in range(dp_count)]
    behind = [(j, i) for i, j in ahead]
    model_width = gate_weight.shape[1]
    shard_width = gate_weight.shape[0]
    half_width = model_width // 2
    tile_rows, tile_cols, inner = queries.shape
    core = lax.axis_index("col") % 2

    peer_out = lax.ppermute(out_weight, "dp", ahead)

    positions = lax.axis_index(("row", "col")) * shard_width + jnp.arange(shard_width)
    own_row = lax.dynamic_index_in_dim(class_table, label, 0, keepdims=False).astype(F32)
    scalars = jnp.stack([label.astype(F32), step.astype(F32)])
    ask = jnp.concatenate([own_row, scalars, jnp.zeros((62,), F32)])[None]
    asked = lax.ppermute(ask, "dp", behind)[0]
    their_label = asked[shard_width].astype(jnp.int32)
    row_for_them = lax.dynamic_index_in_dim(class_table, their_label, 0, keepdims=False).astype(F32)
    their_cond = cond_shard(asked[:shard_width], row_for_them, asked[shard_width + 1], positions, half_width)
    their_part = jnp.dot(their_cond[None], gate_weight, preferred_element_type=F32)[0]
    answer = jnp.concatenate([their_part, row_for_them, jnp.zeros((64,), F32)]).reshape(17, 128)
    answered = lax.ppermute(answer, "dp", ahead).reshape(-1)
    peer_row = answered[model_width : model_width + shard_width]
    cond = cond_shard(own_row, peer_row, step.astype(F32), positions, half_width)
    own_part = jnp.dot(cond[None], gate_weight, preferred_element_type=F32)[0]
    gate_part = 0.5 * (own_part + answered[:model_width])

    up_pairs = [(i, i + 1) for i in range(row_count - 1)]
    down_pairs = [(j, i) for i, j in up_pairs]
    up = lax.ppermute(keyvals[:, tile_rows - RADIUS :], "row", up_pairs)
    down = lax.ppermute(keyvals[:, :RADIUS], "row", down_pairs)
    near_pairs = [(i, i ^ 1) for i in range(col_count)]
    far_pairs = [(i, i + 1) for i in range(1, col_count - 1, 2)]
    far_pairs = far_pairs + [(j, i) for i, j in far_pairs]

    def edge(lead):
        def cut(array):
            right, left = array[:, :, tile_cols - EDGE :], array[:, :, :EDGE]
            return jnp.where(lead, right, left)

        parts = [cut(up), cut(keyvals), cut(down)]
        parts.append(jnp.zeros((2, PAD_ROWS, EDGE, inner), BF16))
        return jnp.concatenate(parts, axis=1).reshape(2, -1, inner)

    near = lax.ppermute(edge(core == 0), "col", near_pairs)
    far = lax.ppermute(edge(core == 1), "col", far_pairs)
    attended = attend(
        queries.reshape(-1, inner),
        keyvals.reshape(2, -1, inner),
        up.reshape(2, -1, inner),
        down.reshape(2, -1, inner),
        near,
        far,
    )

    mixed = (0.5 * (out_weight.astype(F32) + peer_out.astype(F32))).astype(BF16)
    shard = mixed.shape[0]
    sent = jnp.concatenate([mixed, two_rows(gate_part), jnp.zeros((6, model_width), BF16)], axis=0)
    got = [sent] + [
        lax.ppermute(sent, "row", [(i, (i + k) % row_count) for i in range(row_count)])
        for k in range(1, row_count)
    ]
    gate_rows = sum(summed(part[shard : shard + 2]) for part in got)
    stack = jnp.concatenate(
        [part[:shard] for part in got] + [two_rows(gate_rows), jnp.zeros((6, model_width), BF16)],
        axis=0,
    )
    places = [stack] + [
        lax.ppermute(stack, "col", [(i, (i + 2 * k) % col_count) for i in range(col_count)])
        for k in range(1, col_count // 2)
    ]
    siblings = [lax.ppermute(part, "col", near_pairs) for part in places]
    pieces = places + siblings
    height = shard * row_count
    gate = sum(summed(part[height : height + 2]) for part in pieces)
    result = project(attended, gate[None], pieces)
    return result.reshape(1, tile_rows, tile_cols, model_width)


def local(queries, keyvals, out_weight, gate_weight, class_table, labels, timesteps, round_index):
    bit_count = lax.axis_size("dp").bit_length() - 1

    def branch(power):
        return lambda *args: body(2**power, *args)

    return lax.switch(
        round_index[0] % bit_count,
        [branch(power) for power in range(bit_count)],
        queries[0],
        keyvals[0],
        out_weight[0],
        gate_weight[0],
        class_table[0],
        labels[0],
        timesteps[0],
    )


def solution(mesh):
    placed = (
        P("dp", "row", "col", None),
        P("dp", None, "row", "col", None),
        P("dp", ("row", "col"), None),
        P("dp", ("row", "col"), None),
        P("dp", None, ("row", "col")),
        P("dp"),
        P("dp"),
        P(),
    )
    return jax.shard_map(
        local, mesh=mesh, in_specs=placed, out_specs=P("dp", "row", "col", None), check_vma=False
    )
```

```python
import math

import jax
import jax.numpy as jnp
from jax import lax
from jax.experimental import pallas as pl
from jax.experimental.pallas import tpu as pltpu
from jax.sharding import PartitionSpec as P

HDIM = 128
RADIUS = 3
F32 = jnp.float32
BF16 = jnp.bfloat16
GROUP = 4
EDGE = 4
PAD_ROWS = 2


def attend_kernel(q_ref, kv_ref, up_ref, down_ref, near_ref, far_ref, out_ref):
    rows, cols = 12, 16
    inner = q_ref.shape[1]
    row0 = lax.axis_index("row") * rows
    col_index = lax.axis_index("col")
    col0 = col_index * cols
    core = lax.rem(col_index, 2)
    near_base = jnp.where(core == 0, cols, -EDGE)
    far_base = jnp.where(core == 0, -EDGE, cols)
    queries = GROUP * cols
    band = (GROUP + 2 * RADIUS) * cols
    side = (GROUP + 2 * RADIUS + PAD_ROWS) * EDGE
    keys = band + 2 * side
    halo = RADIUS * cols
    factor = math.log2(math.e) / math.sqrt(HDIM)
    q_id = lax.broadcasted_iota(jnp.int32, (queries, keys), 0)
    k_id = lax.broadcasted_iota(jnp.int32, (queries, keys), 1)
    q_row, q_col = q_id // cols, q_id % cols
    side_id = jnp.where(k_id < band + side, k_id - band, k_id - band - side)
    k_row = jnp.where(k_id < band, k_id // cols, side_id // EDGE)
    base = jnp.where(k_id < band + side, near_base, far_base)
    k_col = jnp.where(k_id < band, k_id % cols, base + side_id % EDGE)
    d_row, d_col = k_row - q_row, k_col - q_col
    reach = (d_row >= 0) & (d_row <= 2 * RADIUS) & (d_col >= -RADIUS) & (d_col <= RADIUS)
    k_gcol = col0 + k_col
    reach = reach & (k_gcol >= 0) & (k_gcol < cols * lax.axis_size("col"))
    ones = jnp.ones((keys, HDIM), BF16)
    for group in range(rows // GROUP):
        k_grow = row0 + GROUP * group - RADIUS + k_row
        allowed = reach & (k_grow >= 0) & (k_grow < rows * lax.axis_size("row"))
        bias = jnp.where(allowed, F32(0.0), F32(-1e30))
        first = (GROUP * group - RADIUS) * cols
        last = first + band
        for head in range(inner // HDIM):
            lanes = slice(head * HDIM, (head + 1) * HDIM)

            def gathered(which):
                parts = []
                if first < 0:
                    parts.append(up_ref[which, halo + first : halo, lanes])
                parts.append(kv_ref[which, max(first, 0) : min(last, rows * cols), lanes])
                if last > rows * cols:
                    parts.append(down_ref[which, 0 : last - rows * cols, lanes])
                span = slice(GROUP * group * EDGE, GROUP * group * EDGE + side)
                parts.append(near_ref[which, span, lanes])
                parts.append(far_ref[which, span, lanes])
                return jnp.concatenate(parts, axis=0)

            q = q_ref[group * queries : (group + 1) * queries, lanes]
            scores = lax.dot_general(
                q, gathered(0), (((1,), (1,)), ((), ())), preferred_element_type=F32
            )
            scores = scores + bias
            top = jnp.max(scores, axis=-1, keepdims=True)
            weight = jnp.exp2((scores - top) * factor).astype(BF16)
            values = jnp.concatenate([gathered(1), ones], axis=1)
            both = jnp.dot(weight, values, preferred_element_type=F32)
            out_ref[group * queries : (group + 1) * queries, lanes] = (
                both[:, :HDIM] / both[:, HDIM:]
            ).astype(BF16)


def attend(q, kv, up, down, near, far):
    tokens, inner = q.shape
    return pl.pallas_call(
        attend_kernel,
        out_shape=jax.ShapeDtypeStruct((tokens, inner), BF16),
        in_specs=[pl.BlockSpec(memory_space=pltpu.VMEM)] * 6,
        out_specs=pl.BlockSpec(memory_space=pltpu.VMEM),
        compiler_params=pltpu.CompilerParams(vmem_limit_bytes=20 * 2**20),
        cost_estimate=pl.CostEstimate(flops=1_200_000_000, bytes_accessed=3_000_000, transcendentals=400_000),
        name="attend",
    )(q, kv, up, down, near, far)


def in_vmem(count):
    return [pl.BlockSpec(memory_space=pltpu.VMEM)] * count


def picked_row(label, table):
    ids = lax.broadcasted_iota(jnp.int32, (16, table.shape[0]), 1).astype(F32)
    one_hot = jnp.where(ids == label, F32(1.0), F32(0.0)).astype(BF16)
    return jnp.dot(one_hot, table, preferred_element_type=F32)


def gate_product(row_a, row_b, embed, gate_weight):
    value = (0.5 * (row_a + row_b)).astype(BF16).astype(F32) + embed
    cond = (value / (1.0 + jnp.exp(-value))).astype(BF16)
    return jnp.dot(cond, gate_weight, preferred_element_type=F32)


def begin_kernel(label_ref, embed_ref, table_ref, kv_ref, ask_ref, low_ref, high_ref, sems):
    tokens, halo = kv_ref.shape[1], low_ref.shape[1]
    lower = pltpu.make_async_copy(kv_ref.at[:, pl.ds(tokens - halo, halo), :], low_ref, sems.at[0])
    upper = pltpu.make_async_copy(kv_ref.at[:, pl.ds(0, halo), :], high_ref, sems.at[1])
    lower.start()
    upper.start()
    label = jnp.full((1, 1), label_ref[0], jnp.int32).astype(F32)
    row = picked_row(label, table_ref[...])[:1]
    ask_ref[:, 0:128] = jnp.concatenate([row, embed_ref[...]], axis=1)
    ask_ref[:, 128:256] = jnp.broadcast_to(label, (1, 128))
    lower.wait()
    upper.wait()


def begin(label, embed, table, kv):
    inner = kv.shape[2]
    halo = RADIUS * 16
    edge = jax.ShapeDtypeStruct((2, halo, inner), BF16)
    return pl.pallas_call(
        begin_kernel,
        out_shape=(jax.ShapeDtypeStruct((1, 256), F32), edge, edge),
        in_specs=[pl.BlockSpec(memory_space=pltpu.SMEM)] + in_vmem(2) + [pl.BlockSpec(memory_space=pl.ANY)],
        out_specs=tuple(in_vmem(3)),
        scratch_shapes=[pltpu.SemaphoreType.DMA((2,))],
        compiler_params=pltpu.CompilerParams(vmem_limit_bytes=8 * 2**20),
        name="begin",
    )(label, embed, table, kv)


def answer_kernel(asked_ref, table_ref, gate_ref, answer_ref):
    width = gate_ref.shape[1]
    row = picked_row(asked_ref[:, 128:129], table_ref[...])
    part = gate_product(row, asked_ref[:, 0:64], asked_ref[:, 64:128], gate_ref[...])
    answer_ref[:, 0:width] = part[:1]
    answer_ref[:, width:] = jnp.concatenate([row[:1], row[:1]], axis=1)


def answer(asked, table, gate_weight):
    return pl.pallas_call(
        answer_kernel,
        out_shape=jax.ShapeDtypeStruct((1, gate_weight.shape[1] + 128), F32),
        in_specs=in_vmem(3),
        out_specs=pl.BlockSpec(memory_space=pltpu.VMEM),
        compiler_params=pltpu.CompilerParams(vmem_limit_bytes=8 * 2**20),
        name="answer",
    )(asked, table, gate_weight)


def two_rows(value):
    high = value.astype(BF16).astype(F32)
    ids = lax.broadcasted_iota(jnp.int32, (8, value.shape[1]), 0)
    return jnp.where(ids == 0, high, jnp.where(ids == 1, value - high, F32(0.0))).astype(BF16)


def mix_kernel(own_ref, peer_ref, ask_ref, answered_ref, gate_ref, sent_ref):
    shard, width = own_ref.shape
    sent_ref[0:shard, :] = (0.5 * (own_ref[...].astype(F32) + peer_ref[...].astype(F32))).astype(BF16)
    own_row = jnp.broadcast_to(ask_ref[:, 0:64], (16, 64))
    part = gate_product(own_row, answered_ref[:, width : width + 64], ask_ref[:, 64:128], gate_ref[...])
    sent_ref[shard : shard + 8, :] = two_rows(0.5 * (part[:1] + answered_ref[:, 0:width]))


def mix(own, peer, ask, answered, gate_weight):
    shard, width = own.shape
    return pl.pallas_call(
        mix_kernel,
        out_shape=jax.ShapeDtypeStruct((shard + 8, width), BF16),
        in_specs=in_vmem(5),
        out_specs=pl.BlockSpec(memory_space=pltpu.VMEM),
        compiler_params=pltpu.CompilerParams(vmem_limit_bytes=8 * 2**20),
        name="mix",
    )(own, peer, ask, answered, gate_weight)


def stack_kernel(*refs):
    parts, out_ref = refs[:4], refs[4]
    shard = parts[0].shape[0] - 8
    total = jnp.zeros((8, out_ref.shape[1]), F32)
    for index, part in enumerate(parts):
        out_ref[index * shard : (index + 1) * shard, :] = part[0:shard, :]
        total = total + part[shard : shard + 8, :].astype(F32)
    out_ref[4 * shard : 4 * shard + 8, :] = two_rows(jnp.sum(total, axis=0, keepdims=True))


def stacked(parts):
    rows, width = parts[0].shape
    return pl.pallas_call(
        stack_kernel,
        out_shape=jax.ShapeDtypeStruct((4 * (rows - 8) + 8, width), BF16),
        in_specs=in_vmem(4),
        out_specs=pl.BlockSpec(memory_space=pltpu.VMEM),
        compiler_params=pltpu.CompilerParams(vmem_limit_bytes=8 * 2**20),
        name="stack",
    )(*parts)


def edges_kernel(kv_ref, up_ref, down_ref, near_ref, far_ref):
    cols = 16
    core = lax.rem(lax.axis_index("col"), 2)
    count = near_ref.shape[1]
    source = up_ref.shape[1] + kv_ref.shape[1] + down_ref.shape[1]
    out_id = lax.broadcasted_iota(jnp.int32, (count, source), 0)
    in_id = lax.broadcasted_iota(jnp.int32, (count, source), 1)
    right = (out_id // EDGE) * cols + cols - EDGE + out_id % EDGE
    left = (out_id // EDGE) * cols + out_id % EDGE
    right = jnp.where(in_id == right, F32(1.0), F32(0.0))
    left = jnp.where(in_id == left, F32(1.0), F32(0.0))
    first = core == 0
    pick_near = jnp.where(first, right, left).astype(BF16)
    pick_far = jnp.where(first, left, right).astype(BF16)
    for which in range(2):
        tall = jnp.concatenate([up_ref[which], kv_ref[which], down_ref[which]], axis=0)
        near_ref[which] = jnp.dot(pick_near, tall, preferred_element_type=F32).astype(BF16)
        far_ref[which] = jnp.dot(pick_far, tall, preferred_element_type=F32).astype(BF16)


def edges(kv, up, down):
    inner = kv.shape[2]
    count = (12 + 2 * RADIUS + PAD_ROWS) * EDGE
    edge = jax.ShapeDtypeStruct((2, count, inner), BF16)
    return pl.pallas_call(
        edges_kernel,
        out_shape=(edge, edge),
        in_specs=in_vmem(3),
        out_specs=tuple(in_vmem(2)),
        compiler_params=pltpu.CompilerParams(vmem_limit_bytes=12 * 2**20),
        name="edges",
    )(kv, up, down)


def project_kernel(a_ref, *refs):
    pieces, (out_ref, lanes_ref, held_ref, sems) = refs[:8], refs[8:]
    row, col = lax.axis_index("row"), lax.axis_index("col")
    core, place = lax.rem(col, 2), lax.div(col, 2)
    shard, block = 32, 256
    tokens, width = a_ref.shape[0], out_ref.shape[1]
    for back in range(4):
        start = pl.multiple_of(lax.rem(row + 4 - back, 4) * block, block)
        lanes = a_ref[:, pl.ds(start, block)].astype(F32)
        lanes = pltpu.roll(lanes, block - 64 * place, 1).astype(BF16)
        for step in range(4):
            at = ((4 - step) % 4) * 64
            lanes_ref[:, step * block + back * 64 : step * block + (back + 1) * 64] = lanes[:, at : at + 64]
    total = jnp.zeros((8, width), F32)
    for piece in pieces:
        total = total + piece[4 * shard : 4 * shard + 8, :].astype(F32)
    gate = jnp.sum(total, axis=0, keepdims=True)
    part_width = 512
    parts = width // part_width

    def multiply(even, odd):
        for part in range(parts):
            at = slice(part * part_width, (part + 1) * part_width)
            rows = []
            for step in range(4):
                for back in range(4):
                    span = slice(back * shard, (back + 1) * shard)
                    rows += [even[step][span, at], odd[step][span, at]]
            product = jnp.dot(lanes_ref[...], jnp.concatenate(rows, axis=0), preferred_element_type=F32)
            held_ref[:, at] = (gate[:, at] * product).astype(BF16)
            copy_out(part).start()

    def copy_out(part):
        at = pl.ds(part * part_width, part_width)
        return pltpu.make_async_copy(held_ref.at[:, at], out_ref.at[:, at], sems.at[part])

    @pl.when(core == 0)
    def _():
        multiply(pieces[:4], pieces[4:])

    @pl.when(core == 1)
    def _():
        multiply(pieces[4:], pieces[:4])

    for part in range(parts):
        copy_out(part).wait()


def project(a, pieces):
    tokens, inner = a.shape
    width = pieces[0].shape[1]
    return pl.pallas_call(
        project_kernel,
        out_shape=jax.ShapeDtypeStruct((tokens, width), BF16),
        in_specs=in_vmem(9),
        out_specs=pl.BlockSpec(memory_space=pltpu.HBM),
        scratch_shapes=[
            pltpu.VMEM((tokens, inner), BF16),
            pltpu.VMEM((tokens, width), BF16),
            pltpu.SemaphoreType.DMA((4,)),
        ],
        compiler_params=pltpu.CompilerParams(vmem_limit_bytes=24 * 2**20),
        cost_estimate=pl.CostEstimate(flops=810_000_000, bytes_accessed=6_000_000, transcendentals=0),
        name="project",
    )(a, *pieces)


def time_embed(step, shard_width, model_width):
    half_width = model_width // 2
    positions = lax.axis_index(("row", "col")) * shard_width + jnp.arange(shard_width)
    freq_index = (positions % half_width).astype(F32)
    frequency = jnp.exp(-math.log(10000.0) * freq_index / half_width)
    angle = step.astype(F32) * frequency
    return jnp.where(positions < half_width, jnp.cos(angle), jnp.sin(angle))[None]


def body(distance, queries, keyvals, out_weight, gate_weight, class_table, label, step):
    dp_count, row_count, col_count = (lax.axis_size(a) for a in ("dp", "row", "col"))
    ahead = [(i, (i + distance) % dp_count) for i in range(dp_count)]
    behind = [(j, i) for i, j in ahead]
    tile_rows, tile_cols, inner = queries.shape
    kv = keyvals.reshape(2, -1, inner)

    embed = time_embed(step[0], gate_weight.shape[0], gate_weight.shape[1])
    ask, low, high = begin(label, embed, class_table, kv)
    asked = lax.ppermute(ask, "dp", behind)
    peer_out = lax.ppermute(out_weight, "dp", ahead)
    up_pairs = [(i, i + 1) for i in range(row_count - 1)]
    up = lax.ppermute(low, "row", up_pairs)
    down = lax.ppermute(high, "row", [(j, i) for i, j in up_pairs])
    answered = lax.ppermute(answer(asked, class_table, gate_weight), "dp", ahead)
    near_pairs = [(i, i ^ 1) for i in range(col_count)]
    far_pairs = [(i, i + 1) for i in range(1, col_count - 1, 2)]
    near, far = edges(kv, up, down)
    near = lax.ppermute(near, "col", near_pairs)
    far = lax.ppermute(far, "col", far_pairs + [(j, i) for i, j in far_pairs])

    sent = mix(out_weight, peer_out, ask, answered, gate_weight)
    sent, near, far = lax.optimization_barrier((sent, near, far))
    got = [sent] + [
        lax.ppermute(sent, "row", [(i, (i + k) % row_count) for i in range(row_count)])
        for k in range(1, row_count)
    ]
    attended = attend(queries.reshape(-1, inner), kv, up, down, near, far)
    stack, attended = lax.optimization_barrier((stacked(got), attended))
    places = [stack] + [
        lax.ppermute(stack, "col", [(i, (i + 2 * k) % col_count) for i in range(col_count)])
        for k in range(1, col_count // 2)
    ]
    siblings = [lax.ppermute(part, "col", near_pairs) for part in places]
    result = project(attended, places + siblings)
    return result.reshape(1, tile_rows, tile_cols, -1)


def local(queries, keyvals, out_weight, gate_weight, class_table, labels, timesteps, round_index):
    bit_count = lax.axis_size("dp").bit_length() - 1

    def branch(power):
        return lambda *args: body(2**power, *args)

    return lax.switch(
        round_index[0] % bit_count,
        [branch(power) for power in range(bit_count)],
        queries[0],
        keyvals[0],
        out_weight[0],
        gate_weight[0],
        class_table[0],
        labels,
        timesteps,
    )


def solution(mesh):
    placed = (
        P("dp", "row", "col", None),
        P("dp", None, "row", "col", None),
        P("dp", ("row", "col"), None),
        P("dp", ("row", "col"), None),
        P("dp", None, ("row", "col")),
        P("dp"),
        P("dp"),
        P(),
    )
    return jax.shard_map(
        local, mesh=mesh, in_specs=placed, out_specs=P("dp", "row", "col", None), check_vma=False
    )
```

```python
import math

import jax
import jax.numpy as jnp
from jax import lax
from jax.experimental import pallas as pl
from jax.experimental.pallas import tpu as pltpu
from jax.sharding import PartitionSpec as P

HDIM = 128
RADIUS = 3
F32 = jnp.float32
BF16 = jnp.bfloat16
GROUP = 4
EDGE = 4
PAD_ROWS = 2


def attend_kernel(q_ref, kv_ref, up_ref, down_ref, near_ref, far_ref, out_ref):
    rows, cols = 12, 16
    inner = q_ref.shape[1]
    row0 = lax.axis_index("row") * rows
    col_index = lax.axis_index("col")
    col0 = col_index * cols
    core = lax.rem(col_index, 2)
    near_base = jnp.where(core == 0, cols, -EDGE)
    far_base = jnp.where(core == 0, -EDGE, cols)
    queries = GROUP * cols
    band = (GROUP + 2 * RADIUS) * cols
    side = (GROUP + 2 * RADIUS + PAD_ROWS) * EDGE
    keys = band + 2 * side
    halo = RADIUS * cols
    factor = math.log2(math.e) / math.sqrt(HDIM)
    q_id = lax.broadcasted_iota(jnp.int32, (queries, keys), 0)
    k_id = lax.broadcasted_iota(jnp.int32, (queries, keys), 1)
    q_row, q_col = q_id // cols, q_id % cols
    side_id = jnp.where(k_id < band + side, k_id - band, k_id - band - side)
    k_row = jnp.where(k_id < band, k_id // cols, side_id // EDGE)
    base = jnp.where(k_id < band + side, near_base, far_base)
    k_col = jnp.where(k_id < band, k_id % cols, base + side_id % EDGE)
    d_row, d_col = k_row - q_row, k_col - q_col
    reach = (d_row >= 0) & (d_row <= 2 * RADIUS) & (d_col >= -RADIUS) & (d_col <= RADIUS)
    k_gcol = col0 + k_col
    reach = reach & (k_gcol >= 0) & (k_gcol < cols * lax.axis_size("col"))
    ones = jnp.ones((keys, HDIM), BF16)
    for group in range(rows // GROUP):
        k_grow = row0 + GROUP * group - RADIUS + k_row
        allowed = reach & (k_grow >= 0) & (k_grow < rows * lax.axis_size("row"))
        bias = jnp.where(allowed, F32(0.0), F32(-1e30))
        first = (GROUP * group - RADIUS) * cols
        last = first + band
        for head in range(inner // HDIM):
            lanes = slice(head * HDIM, (head + 1) * HDIM)

            def gathered(which):
                parts = []
                if first < 0:
                    parts.append(up_ref[which, halo + first : halo, lanes])
                parts.append(kv_ref[which, max(first, 0) : min(last, rows * cols), lanes])
                if last > rows * cols:
                    parts.append(down_ref[which, 0 : last - rows * cols, lanes])
                span = slice(GROUP * group * EDGE, GROUP * group * EDGE + side)
                parts.append(near_ref[which, span, lanes])
                parts.append(far_ref[which, span, lanes])
                return jnp.concatenate(parts, axis=0)

            q = q_ref[group * queries : (group + 1) * queries, lanes]
            scores = lax.dot_general(
                q, gathered(0), (((1,), (1,)), ((), ())), preferred_element_type=F32
            )
            scores = scores + bias
            top = jnp.max(scores, axis=-1, keepdims=True)
            weight = jnp.exp2((scores - top) * factor).astype(BF16)
            values = jnp.concatenate([gathered(1), ones], axis=1)
            both = jnp.dot(weight, values, preferred_element_type=F32)
            out_ref[group * queries : (group + 1) * queries, lanes] = (
                both[:, :HDIM] / both[:, HDIM:]
            ).astype(BF16)


def attend(q, kv, up, down, near, far):
    tokens, inner = q.shape
    return pl.pallas_call(
        attend_kernel,
        out_shape=jax.ShapeDtypeStruct((tokens, inner), BF16),
        in_specs=[pl.BlockSpec(memory_space=pltpu.VMEM)] * 6,
        out_specs=pl.BlockSpec(memory_space=pltpu.VMEM),
        compiler_params=pltpu.CompilerParams(vmem_limit_bytes=20 * 2**20),
        cost_estimate=pl.CostEstimate(flops=1_200_000_000, bytes_accessed=3_000_000, transcendentals=400_000),
        name="attend",
    )(q, kv, up, down, near, far)


def in_vmem(count):
    return [pl.BlockSpec(memory_space=pltpu.VMEM)] * count


def picked_row(label, table):
    ids = lax.broadcasted_iota(jnp.int32, (16, table.shape[1]), 1).astype(F32)
    one_hot = jnp.where(ids == label, F32(1.0), F32(0.0)).astype(BF16)
    return lax.dot_general(one_hot, table, (((1,), (1,)), ((), ())), preferred_element_type=F32)


def gate_product(row_a, row_b, embed, gate_weight):
    value = (0.5 * (row_a + row_b)).astype(BF16).astype(F32) + embed
    cond = (value / (1.0 + jnp.exp(-value))).astype(BF16)
    part = jnp.dot(cond, gate_weight, preferred_element_type=F32)
    return jnp.concatenate([part[:1, at * 128 : (at + 1) * 128] for at in range(16)], axis=0)


def to_block(value):
    high = value.astype(BF16).astype(F32)
    return jnp.concatenate([high, value - high], axis=0).astype(BF16)


def from_block(block):
    block = block.astype(F32)
    return block[:16] + block[16:]


def begin_kernel(label_ref, embed_ref, table_ref, ask_ref):
    label = jnp.full((1, 1), label_ref[0], jnp.int32).astype(F32)
    row = picked_row(label, table_ref[...])[:1]
    ask_ref[:, 0:128] = jnp.concatenate([row, embed_ref[...]], axis=1)
    ask_ref[:, 128:256] = jnp.broadcast_to(label, (1, 128))


def begin(label, embed, table):
    return pl.pallas_call(
        begin_kernel,
        out_shape=jax.ShapeDtypeStruct((1, 256), F32),
        in_specs=[pl.BlockSpec(memory_space=pltpu.SMEM)] + in_vmem(2),
        out_specs=pl.BlockSpec(memory_space=pltpu.VMEM),
        compiler_params=pltpu.CompilerParams(vmem_limit_bytes=8 * 2**20),
        name="begin",
    )(label, embed, table)


def answer_kernel(asked_ref, table_ref, gate_ref, own_ref, answer_ref):
    shard, width = own_ref.shape
    answer_ref[:, 0:width] = own_ref[...]
    row = picked_row(asked_ref[:, 128:129], table_ref[...])
    part = gate_product(row, asked_ref[:, 0:64], asked_ref[:, 64:128], gate_ref[...])
    answer_ref[:, width : width + 128] = to_block(part)
    rows = jnp.concatenate([row, row], axis=1)
    answer_ref[:, width + 128 : width + 256] = jnp.concatenate([rows, rows], axis=0).astype(BF16)


def answer(asked, table, gate_weight, own):
    shard, width = own.shape
    return pl.pallas_call(
        answer_kernel,
        out_shape=jax.ShapeDtypeStruct((shard, width + 256), BF16),
        in_specs=in_vmem(4),
        out_specs=pl.BlockSpec(memory_space=pltpu.VMEM),
        compiler_params=pltpu.CompilerParams(vmem_limit_bytes=8 * 2**20),
        name="answer",
    )(asked, table, gate_weight, own)


def mix_kernel(own_ref, peer_ref, ask_ref, gate_ref, sent_ref):
    shard, width = own_ref.shape
    peer = peer_ref[:, 0:width].astype(F32)
    sent_ref[:, 0:width] = (0.5 * (own_ref[...].astype(F32) + peer)).astype(BF16)
    own_row = jnp.broadcast_to(ask_ref[:, 0:64], (16, 64))
    peer_row = peer_ref[0:16, width + 128 : width + 192].astype(F32)
    part = gate_product(own_row, peer_row, ask_ref[:, 64:128], gate_ref[...])
    part = 0.5 * (part + from_block(peer_ref[:, width : width + 128]))
    sent_ref[:, width : width + 128] = to_block(part)


def mix(own, peer, ask, gate_weight):
    shard, width = own.shape
    return pl.pallas_call(
        mix_kernel,
        out_shape=jax.ShapeDtypeStruct((shard, width + 128), BF16),
        in_specs=in_vmem(4),
        out_specs=pl.BlockSpec(memory_space=pltpu.VMEM),
        compiler_params=pltpu.CompilerParams(vmem_limit_bytes=8 * 2**20),
        name="mix",
    )(own, peer, ask, gate_weight)


def stack_kernel(*refs):
    parts, out_ref = refs[:4], refs[4]
    shard = parts[0].shape[0]
    for index, part in enumerate(parts):
        out_ref[index * shard : (index + 1) * shard, :] = part[...]


def stacked(parts):
    rows, width = parts[0].shape
    return pl.pallas_call(
        stack_kernel,
        out_shape=jax.ShapeDtypeStruct((4 * rows, width), BF16),
        in_specs=in_vmem(4),
        out_specs=pl.BlockSpec(memory_space=pltpu.VMEM),
        compiler_params=pltpu.CompilerParams(vmem_limit_bytes=8 * 2**20),
        name="stack",
    )(*parts)


def cut_kernel(kv_ref, after_ref, low_ref, high_ref, sems):
    tokens, halo = kv_ref.shape[1], low_ref.shape[1]
    lower = pltpu.make_async_copy(kv_ref.at[:, pl.ds(tokens - halo, halo), :], low_ref, sems.at[0])
    upper = pltpu.make_async_copy(kv_ref.at[:, pl.ds(0, halo), :], high_ref, sems.at[1])
    lower.start()
    upper.start()
    lower.wait()
    upper.wait()


def cut(kv, after):
    edge = jax.ShapeDtypeStruct((2, RADIUS * 16, kv.shape[2]), BF16)
    return pl.pallas_call(
        cut_kernel,
        out_shape=(edge, edge),
        in_specs=[pl.BlockSpec(memory_space=pl.ANY)] * 2,
        out_specs=tuple(in_vmem(2)),
        scratch_shapes=[pltpu.SemaphoreType.DMA((2,))],
        compiler_params=pltpu.CompilerParams(vmem_limit_bytes=8 * 2**20),
        name="cut",
    )(kv, after)


def edges_kernel(kv_ref, up_ref, down_ref, after_ref, near_ref, far_ref):
    cols = 16
    core = lax.rem(lax.axis_index("col"), 2)
    count = near_ref.shape[1]
    source = up_ref.shape[1] + kv_ref.shape[1] + down_ref.shape[1]
    out_id = lax.broadcasted_iota(jnp.int32, (count, source), 0)
    in_id = lax.broadcasted_iota(jnp.int32, (count, source), 1)
    right = (out_id // EDGE) * cols + cols - EDGE + out_id % EDGE
    left = (out_id // EDGE) * cols + out_id % EDGE
    right = jnp.where(in_id == right, F32(1.0), F32(0.0))
    left = jnp.where(in_id == left, F32(1.0), F32(0.0))
    first = core == 0
    pick_near = jnp.where(first, right, left).astype(BF16)
    pick_far = jnp.where(first, left, right).astype(BF16)
    for which in range(2):
        tall = jnp.concatenate([up_ref[which], kv_ref[which], down_ref[which]], axis=0)
        near_ref[which] = jnp.dot(pick_near, tall, preferred_element_type=F32).astype(BF16)
        far_ref[which] = jnp.dot(pick_far, tall, preferred_element_type=F32).astype(BF16)


def edges(kv, up, down, after):
    inner = kv.shape[2]
    count = (12 + 2 * RADIUS + PAD_ROWS) * EDGE
    edge = jax.ShapeDtypeStruct((2, count, inner), BF16)
    return pl.pallas_call(
        edges_kernel,
        out_shape=(edge, edge),
        in_specs=in_vmem(3) + [pl.BlockSpec(memory_space=pl.ANY)],
        out_specs=tuple(in_vmem(2)),
        compiler_params=pltpu.CompilerParams(vmem_limit_bytes=12 * 2**20),
        name="edges",
    )(kv, up, down, after)


def project_kernel(a_ref, *refs):
    pieces, (out_ref, lanes_ref, held_ref, sems) = refs[:8], refs[8:]
    row, col = lax.axis_index("row"), lax.axis_index("col")
    core, place = lax.rem(col, 2), lax.div(col, 2)
    shard, block = 32, 256
    tokens, width = a_ref.shape[0], out_ref.shape[1]
    odd_place, high_place = place & 1, place >= 2
    for back in range(4):
        start = pl.multiple_of((row ^ back) * block, block)
        lanes = a_ref[:, pl.ds(start, block)].astype(F32)
        first, second = lanes[:, :128], lanes[:, 128:]
        halves = jnp.where(high_place, second, first), jnp.where(high_place, first, second)
        halves = [pltpu.roll(half, 64 * odd_place, 1).astype(BF16) for half in halves]
        for step in range(4):
            at = (step % 2) * 64
            lanes_ref[:, step * block + back * 64 : step * block + (back + 1) * 64] = halves[step // 2][:, at : at + 64]
    total = jnp.zeros((shard, 128), F32)
    for piece in pieces:
        for back in range(4):
            total = total + piece[back * shard : (back + 1) * shard, width : width + 128].astype(F32)
    total = total[:16] + total[16:]
    gate = jnp.concatenate([total[at : at + 1] for at in range(16)], axis=1)
    part_width = 512
    parts = width // part_width

    def multiply(even, odd):
        for part in range(parts):
            at = slice(part * part_width, (part + 1) * part_width)
            rows = []
            for step in range(4):
                for back in range(4):
                    span = slice(back * shard, (back + 1) * shard)
                    rows += [even[step][span, at], odd[step][span, at]]
            product = jnp.dot(lanes_ref[...], jnp.concatenate(rows, axis=0), preferred_element_type=F32)
            held_ref[:, at] = (gate[:, at] * product).astype(BF16)
            copy_out(part).start()

    def copy_out(part):
        at = pl.ds(part * part_width, part_width)
        return pltpu.make_async_copy(held_ref.at[:, at], out_ref.at[:, at], sems.at[part])

    @pl.when(core == 0)
    def _():
        multiply(pieces[:4], pieces[4:])

    @pl.when(core == 1)
    def _():
        multiply(pieces[4:], pieces[:4])

    for part in range(parts):
        copy_out(part).wait()


def project(a, pieces):
    tokens, inner = a.shape
    width = pieces[0].shape[1] - 128
    return pl.pallas_call(
        project_kernel,
        out_shape=jax.ShapeDtypeStruct((tokens, width), BF16),
        in_specs=in_vmem(9),
        out_specs=pl.BlockSpec(memory_space=pltpu.HBM),
        scratch_shapes=[
            pltpu.VMEM((tokens, inner), BF16),
            pltpu.VMEM((tokens, width), BF16),
            pltpu.SemaphoreType.DMA((4,)),
        ],
        compiler_params=pltpu.CompilerParams(vmem_limit_bytes=24 * 2**20),
        cost_estimate=pl.CostEstimate(flops=810_000_000, bytes_accessed=6_000_000, transcendentals=0),
        name="project",
    )(a, *pieces)


def time_embed(step, shard_width, model_width):
    half_width = model_width // 2
    positions = lax.axis_index(("row", "col")) * shard_width + jnp.arange(shard_width)
    freq_index = (positions % half_width).astype(F32)
    frequency = jnp.exp(-math.log(10000.0) * freq_index / half_width)
    angle = step.astype(F32) * frequency
    return jnp.where(positions < half_width, jnp.cos(angle), jnp.sin(angle))[None]


def local(queries, keyvals, out_weight, gate_weight, class_table, labels, timesteps, round_index):
    dp_count, row_count, col_count = (lax.axis_size(a) for a in ("dp", "row", "col"))
    bit_count = dp_count.bit_length() - 1
    tile_rows, tile_cols, inner = queries.shape[1:]
    kv = keyvals.reshape(2, -1, inner)
    out_weight, gate_weight = out_weight[0], gate_weight[0]
    table = class_table[0].T
    power = round_index[0] % bit_count

    def shifted(value, sign):
        def branch(distance):
            pairs = [(i, (i + sign * distance) % dp_count) for i in range(dp_count)]
            return lambda array: lax.ppermute(array, "dp", pairs)

        return lax.switch(power, [branch(2**bit) for bit in range(bit_count)], value)

    embed = time_embed(timesteps[0], gate_weight.shape[0], gate_weight.shape[1])
    ask = begin(labels, embed, table)
    asked = shifted(ask, -1)
    peer = shifted(answer(asked, table, gate_weight, out_weight), 1)

    sent = mix(out_weight, peer, ask, gate_weight)
    got = [sent] + [
        lax.ppermute(sent, "row", [(i, i ^ k) for i in range(row_count)]) for k in range(1, row_count)
    ]
    stack = stacked(got)
    places = [stack] + [
        lax.ppermute(stack, "col", [(i, i ^ (2 * k)) for i in range(col_count)])
        for k in range(1, col_count // 2)
    ]
    near_pairs = [(i, i ^ 1) for i in range(col_count)]
    siblings = [lax.ppermute(part, "col", near_pairs) for part in places]

    low, high = cut(kv, got[1])
    up_pairs = [(i, i + 1) for i in range(row_count - 1)]
    up = lax.ppermute(low, "row", up_pairs)
    down = lax.ppermute(high, "row", [(j, i) for i, j in up_pairs])
    far_pairs = [(i, i + 1) for i in range(1, col_count - 1, 2)]
    near, far = edges(kv, up, down, places[1])
    near = lax.ppermute(near, "col", near_pairs)
    far = lax.ppermute(far, "col", far_pairs + [(j, i) for i, j in far_pairs])
    attended = attend(queries.reshape(-1, inner), kv, up, down, near, far)
    result = project(attended, places + siblings)
    return result.reshape(1, tile_rows, tile_cols, -1)


def solution(mesh):
    placed = (
        P("dp", "row", "col", None),
        P("dp", None, "row", "col", None),
        P("dp", ("row", "col"), None),
        P("dp", ("row", "col"), None),
        P("dp", None, ("row", "col")),
        P("dp"),
        P("dp"),
        P(),
    )
    return jax.shard_map(
        local, mesh=mesh, in_specs=placed, out_specs=P("dp", "row", "col", None), check_vma=False
    )
```

```python
import functools
import math

import jax
import jax.numpy as jnp
from jax import lax
from jax.experimental import pallas as pl
from jax.experimental.pallas import tpu as pltpu
from jax.sharding import PartitionSpec as P

HDIM = 128
RADIUS = 3
F32 = jnp.float32
BF16 = jnp.bfloat16
GROUP = 4
EDGE = 4
PAD_ROWS = 2


def attend_kernel(q_ref, kv_ref, up_ref, down_ref, near_ref, far_ref, out_ref):
    rows, cols = 12, 16
    inner = q_ref.shape[1]
    row0 = lax.axis_index("row") * rows
    col_index = lax.axis_index("col")
    col0 = col_index * cols
    core = lax.rem(col_index, 2)
    near_base = jnp.where(core == 0, cols, -EDGE)
    far_base = jnp.where(core == 0, -EDGE, cols)
    queries = GROUP * cols
    band = (GROUP + 2 * RADIUS) * cols
    side = (GROUP + 2 * RADIUS + PAD_ROWS) * EDGE
    keys = band + 2 * side
    halo = RADIUS * cols
    factor = math.log2(math.e) / math.sqrt(HDIM)
    q_id = lax.broadcasted_iota(jnp.int32, (queries, keys), 0)
    k_id = lax.broadcasted_iota(jnp.int32, (queries, keys), 1)
    q_row, q_col = q_id // cols, q_id % cols
    side_id = jnp.where(k_id < band + side, k_id - band, k_id - band - side)
    k_row = jnp.where(k_id < band, k_id // cols, side_id // EDGE)
    base = jnp.where(k_id < band + side, near_base, far_base)
    k_col = jnp.where(k_id < band, k_id % cols, base + side_id % EDGE)
    d_row, d_col = k_row - q_row, k_col - q_col
    reach = (d_row >= 0) & (d_row <= 2 * RADIUS) & (d_col >= -RADIUS) & (d_col <= RADIUS)
    k_gcol = col0 + k_col
    reach = reach & (k_gcol >= 0) & (k_gcol < cols * lax.axis_size("col"))
    ones = jnp.ones((keys, HDIM), BF16)
    for group in range(rows // GROUP):
        k_grow = row0 + GROUP * group - RADIUS + k_row
        allowed = reach & (k_grow >= 0) & (k_grow < rows * lax.axis_size("row"))
        bias = jnp.where(allowed, F32(0.0), F32(-1e30))
        first = (GROUP * group - RADIUS) * cols
        last = first + band
        for head in range(inner // HDIM):
            lanes = slice(head * HDIM, (head + 1) * HDIM)

            def gathered(which):
                parts = []
                if first < 0:
                    parts.append(up_ref[which, halo + first : halo, lanes])
                parts.append(kv_ref[which, max(first, 0) : min(last, rows * cols), lanes])
                if last > rows * cols:
                    parts.append(down_ref[which, 0 : last - rows * cols, lanes])
                span = slice(GROUP * group * EDGE, GROUP * group * EDGE + side)
                parts.append(near_ref[which, span, lanes])
                parts.append(far_ref[which, span, lanes])
                return jnp.concatenate(parts, axis=0)

            q = q_ref[group * queries : (group + 1) * queries, lanes]
            scores = lax.dot_general(
                q, gathered(0), (((1,), (1,)), ((), ())), preferred_element_type=F32
            )
            scores = scores + bias
            top = jnp.max(scores, axis=-1, keepdims=True)
            weight = jnp.exp2((scores - top) * factor).astype(BF16)
            values = jnp.concatenate([gathered(1), ones], axis=1)
            both = jnp.dot(weight, values, preferred_element_type=F32)
            out_ref[group * queries : (group + 1) * queries, lanes] = (
                both[:, :HDIM] / both[:, HDIM:]
            ).astype(BF16)


def attend(q, kv, up, down, near, far):
    tokens, inner = q.shape
    return pl.pallas_call(
        attend_kernel,
        out_shape=jax.ShapeDtypeStruct((tokens, inner), BF16),
        in_specs=[pl.BlockSpec(memory_space=pltpu.VMEM)] * 6,
        out_specs=pl.BlockSpec(memory_space=pltpu.VMEM),
        compiler_params=pltpu.CompilerParams(vmem_limit_bytes=20 * 2**20),
        cost_estimate=pl.CostEstimate(flops=3000000000, bytes_accessed=0, transcendentals=0),
        name="attend",
    )(q, kv, up, down, near, far)


def in_vmem(count):
    return [pl.BlockSpec(memory_space=pltpu.VMEM)] * count


def picked_row(label, table):
    ids = lax.broadcasted_iota(jnp.int32, (16, table.shape[1]), 1).astype(F32)
    one_hot = jnp.where(ids == label, F32(1.0), F32(0.0)).astype(BF16)
    return lax.dot_general(one_hot, table, (((1,), (1,)), ((), ())), preferred_element_type=F32)


def gate_product(row_a, row_b, embed, gate_weight):
    value = (0.5 * (row_a + row_b)).astype(BF16).astype(F32) + embed
    cond = (value / (1.0 + jnp.exp(-value))).astype(BF16)
    part = jnp.dot(cond, gate_weight, preferred_element_type=F32)
    return jnp.concatenate([part[:1, at * 128 : (at + 1) * 128] for at in range(16)], axis=0)


def to_block(value):
    high = value.astype(BF16).astype(F32)
    return jnp.concatenate([high, value - high], axis=0).astype(BF16)


def from_block(block):
    block = block.astype(F32)
    return block[:16] + block[16:]


def begin_kernel(label_ref, embed_ref, table_ref, ask_ref):
    label = jnp.full((1, 1), label_ref[0], jnp.int32).astype(F32)
    row = picked_row(label, table_ref[...])[:1]
    ask_ref[:, 0:128] = jnp.concatenate([row, embed_ref[...]], axis=1)
    ask_ref[:, 128:256] = jnp.broadcast_to(label, (1, 128))


def begin(label, embed, table):
    return pl.pallas_call(
        begin_kernel,
        out_shape=jax.ShapeDtypeStruct((1, 256), F32),
        in_specs=[pl.BlockSpec(memory_space=pltpu.SMEM)] + in_vmem(2),
        out_specs=pl.BlockSpec(memory_space=pltpu.VMEM),
        compiler_params=pltpu.CompilerParams(vmem_limit_bytes=8 * 2**20),
        name="begin",
    )(label, embed, table)


def answer_kernel(asked_ref, table_ref, gate_ref, answer_ref):
    row = picked_row(asked_ref[:, 128:129], table_ref[...])
    part = gate_product(row, asked_ref[:, 0:64], asked_ref[:, 64:128], gate_ref[...])
    answer_ref[:, 0:128] = to_block(part)
    rows = jnp.concatenate([row, row], axis=1)
    answer_ref[:, 128:256] = jnp.concatenate([rows, rows], axis=0).astype(BF16)


def answer(asked, table, gate_weight):
    return pl.pallas_call(
        answer_kernel,
        out_shape=jax.ShapeDtypeStruct((32, 256), BF16),
        in_specs=in_vmem(3),
        out_specs=pl.BlockSpec(memory_space=pltpu.VMEM),
        compiler_params=pltpu.CompilerParams(vmem_limit_bytes=8 * 2**20),
        cost_estimate=pl.CostEstimate(flops=5000000000, bytes_accessed=0, transcendentals=0),
        name="answer",
    )(asked, table, gate_weight)


def mix_kernel(own_ref, peer_ref, ask_ref, answered_ref, gate_ref, sent_ref):
    shard, width = own_ref.shape
    peer = peer_ref[...].astype(F32)
    sent_ref[:, 0:width] = (0.5 * (own_ref[...].astype(F32) + peer)).astype(BF16)
    own_row = jnp.broadcast_to(ask_ref[:, 0:64], (16, 64))
    peer_row = answered_ref[0:16, 128:192].astype(F32)
    part = gate_product(own_row, peer_row, ask_ref[:, 64:128], gate_ref[...])
    part = 0.5 * (part + from_block(answered_ref[:, 0:128]))
    sent_ref[:, width : width + 128] = to_block(part)


def mix(own, peer, ask, answered, gate_weight):
    shard, width = own.shape
    return pl.pallas_call(
        mix_kernel,
        out_shape=jax.ShapeDtypeStruct((shard, width + 128), BF16),
        in_specs=in_vmem(5),
        out_specs=pl.BlockSpec(memory_space=pltpu.VMEM),
        compiler_params=pltpu.CompilerParams(vmem_limit_bytes=8 * 2**20),
        cost_estimate=pl.CostEstimate(flops=5000000000, bytes_accessed=0, transcendentals=0),
        name="mix",
    )(own, peer, ask, answered, gate_weight)


def stack_kernel(*refs):
    parts, out_ref = [refs[at] for at in (0, 1, 3, 2)], refs[4]
    shard = parts[0].shape[0]
    for index, part in enumerate(parts):
        out_ref[index * shard : (index + 1) * shard, :] = part[...]


def stacked(parts):
    rows, width = parts[0].shape
    return pl.pallas_call(
        stack_kernel,
        out_shape=jax.ShapeDtypeStruct((4 * rows, width), BF16),
        in_specs=in_vmem(4),
        out_specs=pl.BlockSpec(memory_space=pltpu.VMEM),
        compiler_params=pltpu.CompilerParams(vmem_limit_bytes=8 * 2**20),
        cost_estimate=pl.CostEstimate(flops=5000000000, bytes_accessed=0, transcendentals=0),
        name="stack",
    )(*parts)


def cut_kernel(kv_ref, after_ref, low_ref, high_ref, sems):
    tokens, halo = kv_ref.shape[1], low_ref.shape[1]
    lower = pltpu.make_async_copy(kv_ref.at[:, pl.ds(tokens - halo, halo), :], low_ref, sems.at[0])
    upper = pltpu.make_async_copy(kv_ref.at[:, pl.ds(0, halo), :], high_ref, sems.at[1])
    lower.start()
    upper.start()
    lower.wait()
    upper.wait()


def cut(kv, after):
    edge = jax.ShapeDtypeStruct((2, RADIUS * 16, kv.shape[2]), BF16)
    return pl.pallas_call(
        cut_kernel,
        out_shape=(edge, edge),
        in_specs=[pl.BlockSpec(memory_space=pl.ANY)] * 2,
        out_specs=tuple(in_vmem(2)),
        scratch_shapes=[pltpu.SemaphoreType.DMA((2,))],
        compiler_params=pltpu.CompilerParams(vmem_limit_bytes=8 * 2**20),
        name="cut",
    )(kv, after)


def edges_kernel(kv_ref, up_ref, down_ref, after_ref, near_ref, far_ref):
    cols = 16
    core = lax.rem(lax.axis_index("col"), 2)
    count = near_ref.shape[1]
    source = up_ref.shape[1] + kv_ref.shape[1] + down_ref.shape[1]
    out_id = lax.broadcasted_iota(jnp.int32, (count, source), 0)
    in_id = lax.broadcasted_iota(jnp.int32, (count, source), 1)
    right = (out_id // EDGE) * cols + cols - EDGE + out_id % EDGE
    left = (out_id // EDGE) * cols + out_id % EDGE
    right = jnp.where(in_id == right, F32(1.0), F32(0.0))
    left = jnp.where(in_id == left, F32(1.0), F32(0.0))
    first = core == 0
    pick_near = jnp.where(first, right, left).astype(BF16)
    pick_far = jnp.where(first, left, right).astype(BF16)
    for which in range(2):
        tall = jnp.concatenate([up_ref[which], kv_ref[which], down_ref[which]], axis=0)
        near_ref[which] = jnp.dot(pick_near, tall, preferred_element_type=F32).astype(BF16)
        far_ref[which] = jnp.dot(pick_far, tall, preferred_element_type=F32).astype(BF16)


def edges(kv, up, down, after):
    inner = kv.shape[2]
    count = (12 + 2 * RADIUS + PAD_ROWS) * EDGE
    edge = jax.ShapeDtypeStruct((2, count, inner), BF16)
    return pl.pallas_call(
        edges_kernel,
        out_shape=(edge, edge),
        in_specs=in_vmem(3) + [pl.BlockSpec(memory_space=pl.ANY)],
        out_specs=tuple(in_vmem(2)),
        compiler_params=pltpu.CompilerParams(vmem_limit_bytes=12 * 2**20),
        name="edges",
    )(kv, up, down, after)


def project_kernel(a_ref, *refs):
    pieces, (out_ref, lanes_ref) = refs[:8], refs[8:]
    pieces = [pieces[at] for at in (0, 2, 1, 3, 4, 6, 5, 7)]
    row, col = lax.axis_index("row"), lax.axis_index("col")
    core, place = lax.rem(col, 2), lax.div(col, 2)
    shard, block = 32, 256
    tokens, width = a_ref.shape[0], out_ref.shape[1]
    odd_place, high_place = place & 1, place >= 2
    for back in range(4):
        start = pl.multiple_of((row ^ back) * block, block)
        lanes = a_ref[:, pl.ds(start, block)].astype(F32)
        first, second = lanes[:, :128], lanes[:, 128:]
        halves = jnp.where(high_place, second, first), jnp.where(high_place, first, second)
        halves = [pltpu.roll(half, 64 * odd_place, 1).astype(BF16) for half in halves]
        for step in range(4):
            at = (step % 2) * 64
            lanes_ref[:, step * block + back * 64 : step * block + (back + 1) * 64] = halves[step // 2][:, at : at + 64]
    total = jnp.zeros((shard, 128), F32)
    for piece in pieces:
        for back in range(4):
            total = total + piece[back * shard : (back + 1) * shard, width : width + 128].astype(F32)
    total = total[:16] + total[16:]
    gate = jnp.concatenate([total[at : at + 1] for at in range(16)], axis=1)
    part_width = 512
    parts = width // part_width

    def multiply(even, odd):
        for part in range(parts):
            at = slice(part * part_width, (part + 1) * part_width)
            rows = []
            for step in range(4):
                for back in range(4):
                    span = slice(back * shard, (back + 1) * shard)
                    rows += [even[step][span, at], odd[step][span, at]]
            product = jnp.dot(lanes_ref[...], jnp.concatenate(rows, axis=0), preferred_element_type=F32)
            out_ref[:, at] = (gate[:, at] * product).astype(BF16)

    @pl.when(core == 0)
    def _():
        multiply(pieces[:4], pieces[4:])

    @pl.when(core == 1)
    def _():
        multiply(pieces[4:], pieces[:4])


def project(a, pieces):
    tokens, inner = a.shape
    width = pieces[0].shape[1] - 128
    return pl.pallas_call(
        project_kernel,
        out_shape=jax.ShapeDtypeStruct((tokens, width), BF16),
        in_specs=in_vmem(9),
        out_specs=pl.BlockSpec(memory_space=pltpu.VMEM),
        scratch_shapes=[pltpu.VMEM((tokens, inner), BF16)],
        compiler_params=pltpu.CompilerParams(vmem_limit_bytes=24 * 2**20),
        cost_estimate=pl.CostEstimate(flops=810_000_000, bytes_accessed=6_000_000, transcendentals=0),
        name="project",
    )(a, *pieces)


def time_embed(step, shard_width, model_width):
    half_width = model_width // 2
    positions = lax.axis_index(("row", "col")) * shard_width + jnp.arange(shard_width)
    freq_index = (positions % half_width).astype(F32)
    frequency = jnp.exp(-math.log(10000.0) * freq_index / half_width)
    angle = step.astype(F32) * frequency
    return jnp.where(positions < half_width, jnp.cos(angle), jnp.sin(angle))[None]


def local(queries, keyvals, out_weight, gate_weight, class_table, labels, timesteps, round_index):
    dp_count, row_count, col_count = (lax.axis_size(a) for a in ("dp", "row", "col"))
    bit_count = dp_count.bit_length() - 1
    tile_rows, tile_cols, inner = queries.shape[1:]
    up_pairs = [(i, i + 1) for i in range(row_count - 1)]
    down_pairs = [(j, i) for i, j in up_pairs]
    near_pairs = [(i, i ^ 1) for i in range(col_count)]
    far_pairs = [(i, i + 1) for i in range(1, col_count - 1, 2)]
    far_pairs = far_pairs + [(j, i) for i, j in far_pairs]

    def body(distance, ask, table, gate_weight, out_weight, q, kv):
        ahead = [(i, (i + distance) % dp_count) for i in range(dp_count)]
        behind = [(j, i) for i, j in ahead]
        asked = lax.ppermute(ask, "dp", behind)
        peer = lax.ppermute(out_weight, "dp", ahead)
        low, high = cut(kv, ask)
        up = lax.ppermute(low, "row", up_pairs)
        down = lax.ppermute(high, "row", down_pairs)
        answered = lax.ppermute(answer(asked, table, gate_weight), "dp", ahead)
        sent = mix(out_weight, peer, ask, answered, gate_weight)
        got = [sent] + [
            lax.ppermute(sent, "row", [(i, i ^ k) for i in range(row_count)]) for k in (1, 3, 2)
        ]
        stack = stacked(got)
        opposite, beside, other = (
            lax.ppermute(stack, "col", [(i, i ^ (2 * k)) for i in range(col_count)]) for k in (2, 1, 3)
        )
        near, far = edges(kv, up, down, sent)
        far = lax.ppermute(far, "col", far_pairs)
        near = lax.ppermute(near, "col", near_pairs)
        attended = attend(q, kv, up, down, near, far)
        mine, attended = lax.optimization_barrier((stack, attended))
        siblings = [lax.ppermute(part, "col", near_pairs) for part in (mine, opposite, beside, other)]
        return project(attended, [stack, opposite, beside, other] + siblings)

    embed = time_embed(timesteps[0], gate_weight.shape[1], gate_weight.shape[2])
    table = class_table[0].T
    ask = begin(labels, embed, table)
    result = lax.switch(
        round_index[0] % bit_count,
        [functools.partial(body, 2**bit) for bit in range(bit_count)],
        ask,
        table,
        gate_weight[0],
        out_weight[0],
        queries.reshape(-1, inner),
        keyvals.reshape(2, -1, inner),
    )
    return result.reshape(1, tile_rows, tile_cols, -1)


def solution(mesh):
    placed = (
        P("dp", "row", "col", None),
        P("dp", None, "row", "col", None),
        P("dp", ("row", "col"), None),
        P("dp", ("row", "col"), None),
        P("dp", None, ("row", "col")),
        P("dp"),
        P("dp"),
        P(),
    )
    return jax.shard_map(
        local, mesh=mesh, in_specs=placed, out_specs=P("dp", "row", "col", None), check_vma=False
    )
```

```python
import functools
import math

import jax
import jax.numpy as jnp
from jax import lax
from jax.experimental import pallas as pl
from jax.experimental.pallas import tpu as pltpu
from jax.sharding import PartitionSpec as P

HDIM = 128
RADIUS = 3
F32 = jnp.float32
BF16 = jnp.bfloat16
GROUP = 4
EDGE = 4
PAD_ROWS = 2


def attend_kernel(q_ref, kv_ref, up_ref, down_ref, near_ref, far_ref, out_ref):
    rows, cols = 12, 16
    inner = q_ref.shape[1]
    row0 = lax.axis_index("row") * rows
    col_index = lax.axis_index("col")
    col0 = col_index * cols
    core = lax.rem(col_index, 2)
    near_base = jnp.where(core == 0, cols, -EDGE)
    far_base = jnp.where(core == 0, -EDGE, cols)
    queries = GROUP * cols
    band = (GROUP + 2 * RADIUS) * cols
    side = (GROUP + 2 * RADIUS + PAD_ROWS) * EDGE
    keys = band + 2 * side
    halo = RADIUS * cols
    factor = math.log2(math.e) / math.sqrt(HDIM)
    q_id = lax.broadcasted_iota(jnp.int32, (queries, keys), 0)
    k_id = lax.broadcasted_iota(jnp.int32, (queries, keys), 1)
    q_row, q_col = q_id // cols, q_id % cols
    side_id = jnp.where(k_id < band + side, k_id - band, k_id - band - side)
    k_row = jnp.where(k_id < band, k_id // cols, side_id // EDGE)
    base = jnp.where(k_id < band + side, near_base, far_base)
    k_col = jnp.where(k_id < band, k_id % cols, base + side_id % EDGE)
    d_row, d_col = k_row - q_row, k_col - q_col
    reach = (d_row >= 0) & (d_row <= 2 * RADIUS) & (d_col >= -RADIUS) & (d_col <= RADIUS)
    k_gcol = col0 + k_col
    reach = reach & (k_gcol >= 0) & (k_gcol < cols * lax.axis_size("col"))
    ones = jnp.ones((keys, HDIM), BF16)
    for group in range(rows // GROUP):
        k_grow = row0 + GROUP * group - RADIUS + k_row
        allowed = reach & (k_grow >= 0) & (k_grow < rows * lax.axis_size("row"))
        bias = jnp.where(allowed, F32(0.0), F32(-1e30))
        first = (GROUP * group - RADIUS) * cols
        last = first + band
        for head in range(inner // HDIM):
            lanes = slice(head * HDIM, (head + 1) * HDIM)

            def gathered(which):
                parts = []
                if first < 0:
                    parts.append(up_ref[which, halo + first : halo, lanes])
                parts.append(kv_ref[which, max(first, 0) : min(last, rows * cols), lanes])
                if last > rows * cols:
                    parts.append(down_ref[which, 0 : last - rows * cols, lanes])
                span = slice(GROUP * group * EDGE, GROUP * group * EDGE + side)
                parts.append(near_ref[which, span, lanes])
                parts.append(far_ref[which, span, lanes])
                return jnp.concatenate(parts, axis=0)

            q = q_ref[group * queries : (group + 1) * queries, lanes]
            scores = lax.dot_general(
                q, gathered(0), (((1,), (1,)), ((), ())), preferred_element_type=F32
            )
            scores = scores + bias
            top = jnp.max(scores, axis=-1, keepdims=True)
            weight = jnp.exp2((scores - top) * factor).astype(BF16)
            values = jnp.concatenate([gathered(1), ones], axis=1)
            both = jnp.dot(weight, values, preferred_element_type=F32)
            out_ref[group * queries : (group + 1) * queries, lanes] = (
                both[:, :HDIM] / both[:, HDIM:]
            ).astype(BF16)


def attend(q, kv, up, down, near, far):
    tokens, inner = q.shape
    return pl.pallas_call(
        attend_kernel,
        out_shape=jax.ShapeDtypeStruct((tokens, inner), BF16),
        in_specs=[pl.BlockSpec(memory_space=pltpu.VMEM)] * 6,
        out_specs=pl.BlockSpec(memory_space=pltpu.VMEM),
        compiler_params=pltpu.CompilerParams(vmem_limit_bytes=20 * 2**20),
        cost_estimate=pl.CostEstimate(flops=3000000000, bytes_accessed=0, transcendentals=0),
        name="attend",
    )(q, kv, up, down, near, far)


def in_vmem(count):
    return [pl.BlockSpec(memory_space=pltpu.VMEM)] * count


def picked_row(label, table_ref):
    columns, count = table_ref.shape
    kept = jnp.zeros((columns, 128), F32)
    for first in range(0, count, 128):
        width = min(128, count - first)
        block = table_ref[:, first : first + width].astype(F32)
        if width < 128:
            block = jnp.concatenate([block, jnp.zeros((columns, 128 - width), F32)], axis=1)
        ids = lax.broadcasted_iota(jnp.int32, (columns, 128), 1) + first
        kept = kept + jnp.where(ids.astype(F32) == label, block, F32(0.0))
    ones = jnp.ones((16, 128), BF16)
    return lax.dot_general(ones, kept.astype(BF16), (((1,), (1,)), ((), ())), preferred_element_type=F32)


def gate_product(row_a, row_b, embed, gate_weight):
    value = (0.5 * (row_a + row_b)).astype(BF16).astype(F32) + embed
    cond = (value / (1.0 + jnp.exp(-value))).astype(BF16)
    part = jnp.dot(cond, gate_weight, preferred_element_type=F32)
    return jnp.concatenate([part[:1, at * 128 : (at + 1) * 128] for at in range(16)], axis=0)


def to_block(value):
    high = value.astype(BF16).astype(F32)
    return jnp.concatenate([high, value - high], axis=0).astype(BF16)


def from_block(block):
    block = block.astype(F32)
    return block[:16] + block[16:]


def begin_kernel(label_ref, embed_ref, table_ref, gate_ref, ask_ref, table_out, gate_out, sems):
    table_copy = pltpu.make_async_copy(table_ref, table_out, sems.at[0])
    gate_copy = pltpu.make_async_copy(gate_ref, gate_out, sems.at[1])
    table_copy.start()
    gate_copy.start()
    label = jnp.full((1, 1), label_ref[0], jnp.int32).astype(F32)
    table_copy.wait()
    row = picked_row(label, table_out)[:1]
    ask_ref[:, 0:128] = jnp.concatenate([row, embed_ref[...]], axis=1)
    ask_ref[:, 128:256] = jnp.broadcast_to(label, (1, 128))
    gate_copy.wait()


def begin(label, embed, table, gate_weight):
    return pl.pallas_call(
        begin_kernel,
        out_shape=(
            jax.ShapeDtypeStruct((1, 256), F32),
            jax.ShapeDtypeStruct(table.shape, BF16),
            jax.ShapeDtypeStruct(gate_weight.shape, BF16),
        ),
        in_specs=[pl.BlockSpec(memory_space=pltpu.SMEM)] + in_vmem(1) + [pl.BlockSpec(memory_space=pltpu.HBM)] * 2,
        out_specs=tuple(in_vmem(3)),
        scratch_shapes=[pltpu.SemaphoreType.DMA((2,))],
        compiler_params=pltpu.CompilerParams(vmem_limit_bytes=56 * 2**20),
        name="begin",
    )(label, embed, table, gate_weight)


def answer_kernel(asked_ref, table_ref, gate_ref, answer_ref):
    row = picked_row(asked_ref[:, 128:129], table_ref)
    part = gate_product(row, asked_ref[:, 0:64], asked_ref[:, 64:128], gate_ref[...])
    answer_ref[:, 0:128] = to_block(part)
    rows = jnp.concatenate([row, row], axis=1)
    answer_ref[:, 128:256] = jnp.concatenate([rows, rows], axis=0).astype(BF16)


def answer(asked, table, gate_weight):
    return pl.pallas_call(
        answer_kernel,
        out_shape=jax.ShapeDtypeStruct((32, 256), BF16),
        in_specs=in_vmem(3),
        out_specs=pl.BlockSpec(memory_space=pltpu.VMEM),
        compiler_params=pltpu.CompilerParams(vmem_limit_bytes=8 * 2**20),
        cost_estimate=pl.CostEstimate(flops=5000000000, bytes_accessed=0, transcendentals=0),
        name="answer",
    )(asked, table, gate_weight)


def mix_kernel(own_ref, peer_ref, ask_ref, answered_ref, gate_ref, sent_ref):
    shard, width = own_ref.shape
    peer = peer_ref[...].astype(F32)
    sent_ref[:, 0:width] = (0.5 * (own_ref[...].astype(F32) + peer)).astype(BF16)
    own_row = jnp.broadcast_to(ask_ref[:, 0:64], (16, 64))
    peer_row = answered_ref[0:16, 128:192].astype(F32)
    part = gate_product(own_row, peer_row, ask_ref[:, 64:128], gate_ref[...])
    part = 0.5 * (part + from_block(answered_ref[:, 0:128]))
    sent_ref[:, width : width + 128] = to_block(part)


def mix(own, peer, ask, answered, gate_weight):
    shard, width = own.shape
    return pl.pallas_call(
        mix_kernel,
        out_shape=jax.ShapeDtypeStruct((shard, width + 128), BF16),
        in_specs=in_vmem(5),
        out_specs=pl.BlockSpec(memory_space=pltpu.VMEM),
        compiler_params=pltpu.CompilerParams(vmem_limit_bytes=8 * 2**20),
        cost_estimate=pl.CostEstimate(flops=5000000000, bytes_accessed=0, transcendentals=0),
        name="mix",
    )(own, peer, ask, answered, gate_weight)


def stack_kernel(*refs):
    parts, out_ref = [refs[at] for at in (0, 3, 1, 2)], refs[4]
    shard = parts[0].shape[0]
    for index, part in enumerate(parts):
        out_ref[index * shard : (index + 1) * shard, :] = part[...]


def stacked(parts):
    rows, width = parts[0].shape
    return pl.pallas_call(
        stack_kernel,
        out_shape=jax.ShapeDtypeStruct((4 * rows, width), BF16),
        in_specs=in_vmem(4),
        out_specs=pl.BlockSpec(memory_space=pltpu.VMEM),
        compiler_params=pltpu.CompilerParams(vmem_limit_bytes=8 * 2**20),
        cost_estimate=pl.CostEstimate(flops=5000000000, bytes_accessed=0, transcendentals=0),
        name="stack",
    )(*parts)


def cut_kernel(kv_ref, after_ref, low_ref, high_ref, sems):
    tokens, halo = kv_ref.shape[1], low_ref.shape[1]
    lower = pltpu.make_async_copy(kv_ref.at[:, pl.ds(tokens - halo, halo), :], low_ref, sems.at[0])
    upper = pltpu.make_async_copy(kv_ref.at[:, pl.ds(0, halo), :], high_ref, sems.at[1])
    lower.start()
    upper.start()
    lower.wait()
    upper.wait()


def cut(kv, after):
    edge = jax.ShapeDtypeStruct((2, RADIUS * 16, kv.shape[2]), BF16)
    return pl.pallas_call(
        cut_kernel,
        out_shape=(edge, edge),
        in_specs=[pl.BlockSpec(memory_space=pl.ANY)] * 2,
        out_specs=tuple(in_vmem(2)),
        scratch_shapes=[pltpu.SemaphoreType.DMA((2,))],
        compiler_params=pltpu.CompilerParams(vmem_limit_bytes=8 * 2**20),
        name="cut",
    )(kv, after)


def edges_kernel(kv_ref, up_ref, down_ref, after_ref, near_ref, far_ref):
    cols = 16
    core = lax.rem(lax.axis_index("col"), 2)
    count = near_ref.shape[1]
    source = up_ref.shape[1] + kv_ref.shape[1] + down_ref.shape[1]
    out_id = lax.broadcasted_iota(jnp.int32, (count, source), 0)
    in_id = lax.broadcasted_iota(jnp.int32, (count, source), 1)
    right = (out_id // EDGE) * cols + cols - EDGE + out_id % EDGE
    left = (out_id // EDGE) * cols + out_id % EDGE
    right = jnp.where(in_id == right, F32(1.0), F32(0.0))
    left = jnp.where(in_id == left, F32(1.0), F32(0.0))
    first = core == 0
    pick_near = jnp.where(first, right, left).astype(BF16)
    pick_far = jnp.where(first, left, right).astype(BF16)
    for which in range(2):
        tall = jnp.concatenate([up_ref[which], kv_ref[which], down_ref[which]], axis=0)
        near_ref[which] = jnp.dot(pick_near, tall, preferred_element_type=F32).astype(BF16)
        far_ref[which] = jnp.dot(pick_far, tall, preferred_element_type=F32).astype(BF16)


def edges(kv, up, down, after):
    inner = kv.shape[2]
    count = (12 + 2 * RADIUS + PAD_ROWS) * EDGE
    edge = jax.ShapeDtypeStruct((2, count, inner), BF16)
    return pl.pallas_call(
        edges_kernel,
        out_shape=(edge, edge),
        in_specs=in_vmem(3) + [pl.BlockSpec(memory_space=pl.ANY)],
        out_specs=tuple(in_vmem(2)),
        compiler_params=pltpu.CompilerParams(vmem_limit_bytes=12 * 2**20),
        name="edges",
    )(kv, up, down, after)


def weight_rows(even, odd, at):
    rows = []
    for back in range(4):
        span = slice(back * 32, (back + 1) * 32)
        rows += [even[span, at], odd[span, at]]
    return rows


def gate_sum(pieces, width):
    total = jnp.zeros((32, 128), F32)
    for piece in pieces:
        for back in range(4):
            total = total + piece[back * 32 : (back + 1) * 32, width : width + 128].astype(F32)
    return total


def begin_project_kernel(a_ref, own, other, beside, own_x, other_x, beside_x, sum_ref, lanes_ref, gate_ref, held_ref):
    row, col = lax.axis_index("row"), lax.axis_index("col")
    core, place = lax.rem(col, 2), lax.div(col, 2)
    block = 256
    width = sum_ref.shape[1]
    odd_place, high_place = place & 1, place >= 2
    for back in range(4):
        start = pl.multiple_of((row ^ back) * block, block)
        lanes = a_ref[:, pl.ds(start, block)].astype(F32)
        first, second = lanes[:, :128], lanes[:, 128:]
        halves = jnp.where(high_place, second, first), jnp.where(high_place, first, second)
        halves = [pltpu.roll(half, 64 * odd_place, 1).astype(BF16) for half in halves]
        for slot, step in enumerate((0, 1, 3)):
            at = (step % 2) * 64
            held_ref[:, slot * block + back * 64 : slot * block + (back + 1) * 64] = halves[step // 2][:, at : at + 64]
        lanes_ref[:, back * 64 : (back + 1) * 64] = halves[1][:, :64]
    gate_ref[...] = gate_sum((own, beside, other, own_x, beside_x, other_x), width)
    part_width = 512

    def multiply(even, odd):
        for part in range(width // part_width):
            at = slice(part * part_width, (part + 1) * part_width)
            rows = []
            for even_piece, odd_piece in zip(even, odd):
                rows += weight_rows(even_piece, odd_piece, at)
            sum_ref[:, at] = jnp.dot(held_ref[...], jnp.concatenate(rows, axis=0), preferred_element_type=F32)

    @pl.when(core == 0)
    def _():
        multiply((own, beside, other), (own_x, beside_x, other_x))

    @pl.when(core == 1)
    def _():
        multiply((own_x, beside_x, other_x), (own, beside, other))


def begin_project(a, pieces):
    tokens, inner = a.shape
    width = pieces[0].shape[1] - 128
    return pl.pallas_call(
        begin_project_kernel,
        out_shape=(
            jax.ShapeDtypeStruct((tokens, width), F32),
            jax.ShapeDtypeStruct((tokens, inner // 4), BF16),
            jax.ShapeDtypeStruct((32, 128), F32),
        ),
        in_specs=in_vmem(7),
        out_specs=tuple(in_vmem(3)),
        scratch_shapes=[pltpu.VMEM((tokens, inner - inner // 4), BF16)],
        compiler_params=pltpu.CompilerParams(vmem_limit_bytes=20 * 2**20),
        name="begin_project",
    )(a, *pieces)


def project_kernel(sum_ref, lanes_ref, gate_ref, piece, piece_x, out_ref):
    core = lax.rem(lax.axis_index("col"), 2)
    width = out_ref.shape[1]
    total = gate_ref[...] + gate_sum((piece, piece_x), width)
    total = total[:16] + total[16:]
    gate = jnp.concatenate([total[at : at + 1] for at in range(16)], axis=1)
    part_width = 512

    def multiply(even, odd):
        for part in range(width // part_width):
            at = slice(part * part_width, (part + 1) * part_width)
            rows = jnp.concatenate(weight_rows(even, odd, at), axis=0)
            product = jnp.dot(lanes_ref[...], rows, preferred_element_type=F32) + sum_ref[:, at]
            out_ref[:, at] = (gate[:, at] * product).astype(BF16)

    @pl.when(core == 0)
    def _():
        multiply(piece, piece_x)

    @pl.when(core == 1)
    def _():
        multiply(piece_x, piece)


def project(begun, piece, piece_x):
    tokens, width = begun[0].shape
    return pl.pallas_call(
        project_kernel,
        out_shape=jax.ShapeDtypeStruct((tokens, width), BF16),
        in_specs=in_vmem(5),
        out_specs=pl.BlockSpec(memory_space=pltpu.VMEM),
        compiler_params=pltpu.CompilerParams(vmem_limit_bytes=16 * 2**20),
        name="project",
    )(*begun, piece, piece_x)


def time_embed(step, shard_width, model_width):
    half_width = model_width // 2
    positions = lax.axis_index(("row", "col")) * shard_width + jnp.arange(shard_width)
    freq_index = (positions % half_width).astype(F32)
    frequency = jnp.exp(-math.log(10000.0) * freq_index / half_width)
    angle = step.astype(F32) * frequency
    return jnp.where(positions < half_width, jnp.cos(angle), jnp.sin(angle))[None]


def local(queries, keyvals, out_weight, gate_weight, class_table, labels, timesteps, round_index):
    dp_count, row_count, col_count = (lax.axis_size(a) for a in ("dp", "row", "col"))
    bit_count = dp_count.bit_length() - 1
    tile_rows, tile_cols, inner = queries.shape[1:]
    up_pairs = [(i, i + 1) for i in range(row_count - 1)]
    down_pairs = [(j, i) for i, j in up_pairs]
    near_pairs = [(i, i ^ 1) for i in range(col_count)]
    far_pairs = [(i, i + 1) for i in range(1, col_count - 1, 2)]
    far_pairs = far_pairs + [(j, i) for i, j in far_pairs]

    def body(distance, ask, table, gate_weight, out_weight, q, kv):
        ahead = [(i, (i + distance) % dp_count) for i in range(dp_count)]
        behind = [(j, i) for i, j in ahead]
        asked = lax.ppermute(ask, "dp", behind)
        peer = lax.ppermute(out_weight, "dp", ahead)
        low, high = cut(kv, ask)
        up = lax.ppermute(low, "row", up_pairs)
        down = lax.ppermute(high, "row", down_pairs)
        answered = lax.ppermute(answer(asked, table, gate_weight), "dp", ahead)
        sent = mix(out_weight, peer, ask, answered, gate_weight)
        got = [sent] + [
            lax.ppermute(sent, "row", [(i, i ^ k) for i in range(row_count)]) for k in (2, 3, 1)
        ]
        stack = stacked(got)
        opposite, beside, other = (
            lax.ppermute(stack, "col", [(i, i ^ (2 * k)) for i in range(col_count)]) for k in (2, 1, 3)
        )
        near, far = edges(kv, up, down, sent)
        far = lax.ppermute(far, "col", far_pairs)
        near = lax.ppermute(near, "col", near_pairs)
        attended = attend(q, kv, up, down, near, far)
        mine, attended = lax.optimization_barrier((stack, attended))
        siblings = [lax.ppermute(part, "col", near_pairs) for part in (mine, opposite, other, beside)]
        mine_x, opposite_x, other_x, beside_x = siblings
        begun = begin_project(attended, (stack, other, beside, mine_x, other_x, beside_x))
        return project(begun, opposite, opposite_x)

    embed = time_embed(timesteps[0], gate_weight.shape[1], gate_weight.shape[2])
    table = class_table[0].T
    ask, table, gate_weight = begin(labels, embed, table, gate_weight[0])
    result = lax.switch(
        round_index[0] % bit_count,
        [functools.partial(body, 2**bit) for bit in range(bit_count)],
        ask,
        table,
        gate_weight,
        out_weight[0],
        queries.reshape(-1, inner),
        keyvals.reshape(2, -1, inner),
    )
    return result.reshape(1, tile_rows, tile_cols, -1)


def solution(mesh):
    placed = (
        P("dp", "row", "col", None),
        P("dp", None, "row", "col", None),
        P("dp", ("row", "col"), None),
        P("dp", ("row", "col"), None),
        P("dp", None, ("row", "col")),
        P("dp"),
        P("dp"),
        P(),
    )
    return jax.shard_map(
        local, mesh=mesh, in_specs=placed, out_specs=P("dp", "row", "col", None), check_vma=False
    )
```

```python
import functools
import math

import jax
import jax.numpy as jnp
from jax import lax
from jax.experimental import pallas as pl
from jax.experimental.pallas import tpu as pltpu
from jax.sharding import PartitionSpec as P

HDIM = 128
RADIUS = 3
F32 = jnp.float32
BF16 = jnp.bfloat16
GROUP = 4
EDGE = 4
PAD_ROWS = 2


def attend_kernel(q_ref, kv_ref, up_ref, down_ref, near_ref, far_ref, out_ref):
    rows, cols = 12, 16
    inner = q_ref.shape[1]
    row0 = lax.axis_index("row") * rows
    col_index = lax.axis_index("col")
    col0 = col_index * cols
    core = lax.rem(col_index, 2)
    near_base = jnp.where(core == 0, cols, -EDGE)
    far_base = jnp.where(core == 0, -EDGE, cols)
    queries = GROUP * cols
    band = (GROUP + 2 * RADIUS) * cols
    side = (GROUP + 2 * RADIUS + PAD_ROWS) * EDGE
    keys = band + 2 * side
    halo = RADIUS * cols
    factor = math.log2(math.e) / math.sqrt(HDIM)
    q_id = lax.broadcasted_iota(jnp.int32, (queries, keys), 0)
    k_id = lax.broadcasted_iota(jnp.int32, (queries, keys), 1)
    q_row, q_col = q_id // cols, q_id % cols
    side_id = jnp.where(k_id < band + side, k_id - band, k_id - band - side)
    k_row = jnp.where(k_id < band, k_id // cols, side_id // EDGE)
    base = jnp.where(k_id < band + side, near_base, far_base)
    k_col = jnp.where(k_id < band, k_id % cols, base + side_id % EDGE)
    d_row, d_col = k_row - q_row, k_col - q_col
    reach = (d_row >= 0) & (d_row <= 2 * RADIUS) & (d_col >= -RADIUS) & (d_col <= RADIUS)
    k_gcol = col0 + k_col
    reach = reach & (k_gcol >= 0) & (k_gcol < cols * lax.axis_size("col"))
    ones = jnp.ones((keys, HDIM), BF16)
    for group in range(rows // GROUP):
        k_grow = row0 + GROUP * group - RADIUS + k_row
        allowed = reach & (k_grow >= 0) & (k_grow < rows * lax.axis_size("row"))
        bias = jnp.where(allowed, F32(0.0), F32(-1e30))
        first = (GROUP * group - RADIUS) * cols
        last = first + band
        for head in range(inner // HDIM):
            lanes = slice(head * HDIM, (head + 1) * HDIM)

            def gathered(which):
                parts = []
                if first < 0:
                    parts.append(up_ref[which, halo + first : halo, lanes])
                parts.append(kv_ref[which, max(first, 0) : min(last, rows * cols), lanes])
                if last > rows * cols:
                    parts.append(down_ref[which, 0 : last - rows * cols, lanes])
                span = slice(GROUP * group * EDGE, GROUP * group * EDGE + side)
                parts.append(near_ref[which, span, lanes])
                parts.append(far_ref[which, span, lanes])
                return jnp.concatenate(parts, axis=0)

            q = q_ref[group * queries : (group + 1) * queries, lanes]
            scores = lax.dot_general(
                q, gathered(0), (((1,), (1,)), ((), ())), preferred_element_type=F32
            )
            scores = scores + bias
            top = jnp.max(scores, axis=-1, keepdims=True)
            weight = jnp.exp2((scores - top) * factor).astype(BF16)
            values = jnp.concatenate([gathered(1), ones], axis=1)
            both = jnp.dot(weight, values, preferred_element_type=F32)
            out_ref[group * queries : (group + 1) * queries, lanes] = (
                both[:, :HDIM] / both[:, HDIM:]
            ).astype(BF16)


def attend(q, kv, up, down, near, far):
    tokens, inner = q.shape
    return pl.pallas_call(
        attend_kernel,
        out_shape=jax.ShapeDtypeStruct((tokens, inner), BF16),
        in_specs=[pl.BlockSpec(memory_space=pltpu.VMEM)] * 6,
        out_specs=pl.BlockSpec(memory_space=pltpu.VMEM),
        compiler_params=pltpu.CompilerParams(vmem_limit_bytes=20 * 2**20),
        cost_estimate=pl.CostEstimate(flops=3000000000, bytes_accessed=0, transcendentals=0),
        name="attend",
    )(q, kv, up, down, near, far)


def in_vmem(count):
    return [pl.BlockSpec(memory_space=pltpu.VMEM)] * count


def picked_row(label, table_ref):
    columns, count = table_ref.shape
    kept = jnp.zeros((columns, 128), F32)
    for first in range(0, count, 128):
        width = min(128, count - first)
        block = table_ref[:, first : first + width].astype(F32)
        if width < 128:
            block = jnp.concatenate([block, jnp.zeros((columns, 128 - width), F32)], axis=1)
        ids = lax.broadcasted_iota(jnp.int32, (columns, 128), 1) + first
        kept = kept + jnp.where(ids.astype(F32) == label, block, F32(0.0))
    ones = jnp.ones((16, 128), BF16)
    return lax.dot_general(ones, kept.astype(BF16), (((1,), (1,)), ((), ())), preferred_element_type=F32)


def gate_product(row_a, row_b, embed, gate_weight):
    value = (0.5 * (row_a + row_b)).astype(BF16).astype(F32) + embed
    cond = (value / (1.0 + jnp.exp(-value))).astype(BF16)
    part = jnp.dot(cond, gate_weight, preferred_element_type=F32)
    return jnp.concatenate([part[:1, at * 128 : (at + 1) * 128] for at in range(16)], axis=0)


def to_block(value):
    high = value.astype(BF16).astype(F32)
    return jnp.concatenate([high, value - high], axis=0).astype(BF16)


def from_block(block):
    block = block.astype(F32)
    return block[:16] + block[16:]


FETCHES = 4


def begin_kernel(label_ref, step_ref, table_ref, gate_ref, ask_ref, table_out, gate_out, numbers, sems):
    label_copy = pltpu.make_async_copy(label_ref, numbers.at[0], sems.at[2 * FETCHES])
    step_copy = pltpu.make_async_copy(step_ref, numbers.at[1], sems.at[2 * FETCHES + 1])
    label_copy.start()
    step_copy.start()
    copies = []
    for kind, (source, target) in enumerate(((table_ref, table_out), (gate_ref, gate_out))):
        rows = source.shape[0] // FETCHES
        for part in range(FETCHES):
            span = pl.ds(part * rows, rows)
            copies.append(
                pltpu.make_async_copy(source.at[span, :], target.at[span, :], sems.at[kind * FETCHES + part])
            )
            copies[-1].start()
    shard_width, half_width = gate_ref.shape[0], gate_ref.shape[1] // 2
    first = (lax.axis_index("row") * lax.axis_size("col") + lax.axis_index("col")) * shard_width
    positions = lax.broadcasted_iota(jnp.int32, (1, shard_width), 1) + first
    freq_index = jnp.where(positions < half_width, positions, positions - half_width).astype(F32)
    frequency = jnp.exp(-math.log(10000.0) * freq_index / half_width)
    label_copy.wait()
    step_copy.wait()
    angle = jnp.full((1, 1), numbers[1, 0], jnp.int32).astype(F32) * frequency
    embed = jnp.where(positions < half_width, jnp.cos(angle), jnp.sin(angle))
    label = jnp.full((1, 1), numbers[0, 0], jnp.int32).astype(F32)
    for copy in copies[:FETCHES]:
        copy.wait()
    row = picked_row(label, table_out)[:1]
    ask_ref[:, 0:128] = jnp.concatenate([row, embed], axis=1)
    ask_ref[:, 128:256] = jnp.broadcast_to(label, (1, 128))
    for copy in copies[FETCHES:]:
        copy.wait()


def begin(label, step, table, gate_weight):
    return pl.pallas_call(
        begin_kernel,
        out_shape=(
            jax.ShapeDtypeStruct((1, 256), F32),
            jax.ShapeDtypeStruct(table.shape, BF16),
            jax.ShapeDtypeStruct(gate_weight.shape, BF16),
        ),
        in_specs=[pl.BlockSpec(memory_space=pltpu.HBM)] * 4,
        out_specs=tuple(in_vmem(3)),
        scratch_shapes=[pltpu.SMEM((2, 1), jnp.int32), pltpu.SemaphoreType.DMA((2 * FETCHES + 2,))],
        compiler_params=pltpu.CompilerParams(vmem_limit_bytes=56 * 2**20),
        name="begin",
    )(label, step, table, gate_weight)


def answer_kernel(asked_ref, table_ref, gate_ref, answer_ref):
    row = picked_row(asked_ref[:, 128:129], table_ref)
    part = gate_product(row, asked_ref[:, 0:64], asked_ref[:, 64:128], gate_ref[...])
    answer_ref[:, 0:128] = to_block(part)
    rows = jnp.concatenate([row, row], axis=1)
    answer_ref[:, 128:256] = jnp.concatenate([rows, rows], axis=0).astype(BF16)


def answer(asked, table, gate_weight):
    return pl.pallas_call(
        answer_kernel,
        out_shape=jax.ShapeDtypeStruct((32, 256), BF16),
        in_specs=in_vmem(3),
        out_specs=pl.BlockSpec(memory_space=pltpu.VMEM),
        compiler_params=pltpu.CompilerParams(vmem_limit_bytes=8 * 2**20),
        cost_estimate=pl.CostEstimate(flops=5000000000, bytes_accessed=0, transcendentals=0),
        name="answer",
    )(asked, table, gate_weight)


def mix_kernel(own_ref, peer_ref, ask_ref, answered_ref, gate_ref, sent_ref):
    shard, width = own_ref.shape
    peer = peer_ref[...].astype(F32)
    sent_ref[:, 0:width] = (0.5 * (own_ref[...].astype(F32) + peer)).astype(BF16)
    own_row = jnp.broadcast_to(ask_ref[:, 0:64], (16, 64))
    peer_row = answered_ref[0:16, 128:192].astype(F32)
    part = gate_product(own_row, peer_row, ask_ref[:, 64:128], gate_ref[...])
    part = 0.5 * (part + from_block(answered_ref[:, 0:128]))
    sent_ref[:, width : width + 128] = to_block(part)


def mix(own, peer, ask, answered, gate_weight):
    shard, width = own.shape
    return pl.pallas_call(
        mix_kernel,
        out_shape=jax.ShapeDtypeStruct((shard, width + 128), BF16),
        in_specs=in_vmem(5),
        out_specs=pl.BlockSpec(memory_space=pltpu.VMEM),
        compiler_params=pltpu.CompilerParams(vmem_limit_bytes=8 * 2**20),
        cost_estimate=pl.CostEstimate(flops=5000000000, bytes_accessed=0, transcendentals=0),
        name="mix",
    )(own, peer, ask, answered, gate_weight)


def stack_kernel(*refs):
    parts, out_ref = [refs[at] for at in (0, 3, 1, 2)], refs[4]
    shard = parts[0].shape[0]
    for index, part in enumerate(parts):
        out_ref[index * shard : (index + 1) * shard, :] = part[...]


def stacked(parts):
    rows, width = parts[0].shape
    return pl.pallas_call(
        stack_kernel,
        out_shape=jax.ShapeDtypeStruct((4 * rows, width), BF16),
        in_specs=in_vmem(4),
        out_specs=pl.BlockSpec(memory_space=pltpu.VMEM),
        compiler_params=pltpu.CompilerParams(vmem_limit_bytes=8 * 2**20),
        cost_estimate=pl.CostEstimate(flops=5000000000, bytes_accessed=0, transcendentals=0),
        name="stack",
    )(*parts)


def cut_kernel(kv_ref, after_ref, low_ref, high_ref, sems):
    tokens, halo = kv_ref.shape[1], low_ref.shape[1]
    lower = pltpu.make_async_copy(kv_ref.at[:, pl.ds(tokens - halo, halo), :], low_ref, sems.at[0])
    upper = pltpu.make_async_copy(kv_ref.at[:, pl.ds(0, halo), :], high_ref, sems.at[1])
    lower.start()
    upper.start()
    lower.wait()
    upper.wait()


def cut(kv, after):
    edge = jax.ShapeDtypeStruct((2, RADIUS * 16, kv.shape[2]), BF16)
    return pl.pallas_call(
        cut_kernel,
        out_shape=(edge, edge),
        in_specs=[pl.BlockSpec(memory_space=pl.ANY)] * 2,
        out_specs=tuple(in_vmem(2)),
        scratch_shapes=[pltpu.SemaphoreType.DMA((2,))],
        compiler_params=pltpu.CompilerParams(vmem_limit_bytes=8 * 2**20),
        name="cut",
    )(kv, after)


def edges_kernel(kv_ref, up_ref, down_ref, after_ref, near_ref, far_ref):
    cols = 16
    core = lax.rem(lax.axis_index("col"), 2)
    count = near_ref.shape[1]
    source = up_ref.shape[1] + kv_ref.shape[1] + down_ref.shape[1]
    out_id = lax.broadcasted_iota(jnp.int32, (count, source), 0)
    in_id = lax.broadcasted_iota(jnp.int32, (count, source), 1)
    right = (out_id // EDGE) * cols + cols - EDGE + out_id % EDGE
    left = (out_id // EDGE) * cols + out_id % EDGE
    right = jnp.where(in_id == right, F32(1.0), F32(0.0))
    left = jnp.where(in_id == left, F32(1.0), F32(0.0))
    first = core == 0
    pick_near = jnp.where(first, right, left).astype(BF16)
    pick_far = jnp.where(first, left, right).astype(BF16)
    for which in range(2):
        tall = jnp.concatenate([up_ref[which], kv_ref[which], down_ref[which]], axis=0)
        near_ref[which] = jnp.dot(pick_near, tall, preferred_element_type=F32).astype(BF16)
        far_ref[which] = jnp.dot(pick_far, tall, preferred_element_type=F32).astype(BF16)


def edges(kv, up, down, after):
    inner = kv.shape[2]
    count = (12 + 2 * RADIUS + PAD_ROWS) * EDGE
    edge = jax.ShapeDtypeStruct((2, count, inner), BF16)
    return pl.pallas_call(
        edges_kernel,
        out_shape=(edge, edge),
        in_specs=in_vmem(3) + [pl.BlockSpec(memory_space=pl.ANY)],
        out_specs=tuple(in_vmem(2)),
        compiler_params=pltpu.CompilerParams(vmem_limit_bytes=12 * 2**20),
        name="edges",
    )(kv, up, down, after)


def weight_rows(even, odd, at):
    rows = []
    for back in range(4):
        span = slice(back * 32, (back + 1) * 32)
        rows += [even[span, at], odd[span, at]]
    return rows


def gate_sum(pieces, width):
    total = jnp.zeros((32, 128), F32)
    for piece in pieces:
        for back in range(4):
            total = total + piece[back * 32 : (back + 1) * 32, width : width + 128].astype(F32)
    return total


def begin_project_kernel(a_ref, own, other, beside, own_x, other_x, beside_x, sum_ref, lanes_ref, gate_ref, held_ref):
    row, col = lax.axis_index("row"), lax.axis_index("col")
    core, place = lax.rem(col, 2), lax.div(col, 2)
    block = 256
    width = sum_ref.shape[1]
    odd_place, high_place = place & 1, place >= 2
    for back in range(4):
        start = pl.multiple_of((row ^ back) * block, block)
        lanes = a_ref[:, pl.ds(start, block)].astype(F32)
        first, second = lanes[:, :128], lanes[:, 128:]
        halves = jnp.where(high_place, second, first), jnp.where(high_place, first, second)
        halves = [pltpu.roll(half, 64 * odd_place, 1).astype(BF16) for half in halves]
        for slot, step in enumerate((0, 1, 3)):
            at = (step % 2) * 64
            held_ref[:, slot * block + back * 64 : slot * block + (back + 1) * 64] = halves[step // 2][:, at : at + 64]
        lanes_ref[:, back * 64 : (back + 1) * 64] = halves[1][:, :64]
    gate_ref[...] = gate_sum((own, beside, other, own_x, beside_x, other_x), width)
    part_width = 512

    def multiply(even, odd):
        for part in range(width // part_width):
            at = slice(part * part_width, (part + 1) * part_width)
            rows = []
            for even_piece, odd_piece in zip(even, odd):
                rows += weight_rows(even_piece, odd_piece, at)
            sum_ref[:, at] = jnp.dot(held_ref[...], jnp.concatenate(rows, axis=0), preferred_element_type=F32)

    @pl.when(core == 0)
    def _():
        multiply((own, beside, other), (own_x, beside_x, other_x))

    @pl.when(core == 1)
    def _():
        multiply((own_x, beside_x, other_x), (own, beside, other))


def begin_project(a, pieces):
    tokens, inner = a.shape
    width = pieces[0].shape[1] - 128
    return pl.pallas_call(
        begin_project_kernel,
        out_shape=(
            jax.ShapeDtypeStruct((tokens, width), F32),
            jax.ShapeDtypeStruct((tokens, inner // 4), BF16),
            jax.ShapeDtypeStruct((32, 128), F32),
        ),
        in_specs=in_vmem(7),
        out_specs=tuple(in_vmem(3)),
        scratch_shapes=[pltpu.VMEM((tokens, inner - inner // 4), BF16)],
        compiler_params=pltpu.CompilerParams(vmem_limit_bytes=20 * 2**20),
        name="begin_project",
    )(a, *pieces)


def project_kernel(sum_ref, lanes_ref, gate_ref, piece, piece_x, out_ref):
    core = lax.rem(lax.axis_index("col"), 2)
    width = out_ref.shape[1]
    total = gate_ref[...] + gate_sum((piece, piece_x), width)
    total = total[:16] + total[16:]
    gate = jnp.concatenate([total[at : at + 1] for at in range(16)], axis=1)
    part_width = 512

    def multiply(even, odd):
        for part in range(width // part_width):
            at = slice(part * part_width, (part + 1) * part_width)
            rows = jnp.concatenate(weight_rows(even, odd, at), axis=0)
            product = jnp.dot(lanes_ref[...], rows, preferred_element_type=F32) + sum_ref[:, at]
            out_ref[:, at] = (gate[:, at] * product).astype(BF16)

    @pl.when(core == 0)
    def _():
        multiply(piece, piece_x)

    @pl.when(core == 1)
    def _():
        multiply(piece_x, piece)


def project(begun, piece, piece_x):
    tokens, width = begun[0].shape
    return pl.pallas_call(
        project_kernel,
        out_shape=jax.ShapeDtypeStruct((tokens, width), BF16),
        in_specs=in_vmem(5),
        out_specs=pl.BlockSpec(memory_space=pltpu.VMEM),
        compiler_params=pltpu.CompilerParams(vmem_limit_bytes=16 * 2**20),
        name="project",
    )(*begun, piece, piece_x)


def local(queries, keyvals, out_weight, gate_weight, class_table, labels, timesteps, round_index):
    dp_count, row_count, col_count = (lax.axis_size(a) for a in ("dp", "row", "col"))
    bit_count = dp_count.bit_length() - 1
    tile_rows, tile_cols, inner = queries.shape[1:]
    up_pairs = [(i, i + 1) for i in range(row_count - 1)]
    down_pairs = [(j, i) for i, j in up_pairs]
    near_pairs = [(i, i ^ 1) for i in range(col_count)]
    far_pairs = [(i, i + 1) for i in range(1, col_count - 1, 2)]
    far_pairs = far_pairs + [(j, i) for i, j in far_pairs]

    def body(distance, ask, table, gate_weight, out_weight, q, kv):
        ahead = [(i, (i + distance) % dp_count) for i in range(dp_count)]
        behind = [(j, i) for i, j in ahead]
        asked = lax.ppermute(ask, "dp", behind)
        peer = lax.ppermute(out_weight, "dp", ahead)
        low, high = cut(kv, ask)
        up = lax.ppermute(low, "row", up_pairs)
        down = lax.ppermute(high, "row", down_pairs)
        answered = lax.ppermute(answer(asked, table, gate_weight), "dp", ahead)
        sent = mix(out_weight, peer, ask, answered, gate_weight)
        got = [sent] + [
            lax.ppermute(sent, "row", [(i, i ^ k) for i in range(row_count)]) for k in (2, 3, 1)
        ]
        stack = stacked(got)
        opposite, beside, other = (
            lax.ppermute(stack, "col", [(i, i ^ (2 * k)) for i in range(col_count)]) for k in (2, 1, 3)
        )
        near, far = edges(kv, up, down, sent)
        far = lax.ppermute(far, "col", far_pairs)
        near = lax.ppermute(near, "col", near_pairs)
        attended = attend(q, kv, up, down, near, far)
        mine, attended = lax.optimization_barrier((stack, attended))
        siblings = [lax.ppermute(part, "col", near_pairs) for part in (mine, opposite, other, beside)]
        mine_x, opposite_x, other_x, beside_x = siblings
        begun = begin_project(attended, (stack, other, beside, mine_x, other_x, beside_x))
        return project(begun, opposite, opposite_x)

    table = class_table[0].T
    ask, table, gate_weight = begin(labels, timesteps, table, gate_weight[0])
    result = lax.switch(
        round_index[0] % bit_count,
        [functools.partial(body, 2**bit) for bit in range(bit_count)],
        ask,
        table,
        gate_weight,
        out_weight[0],
        queries.reshape(-1, inner),
        keyvals.reshape(2, -1, inner),
    )
    return result.reshape(1, tile_rows, tile_cols, -1)


def solution(mesh):
    placed = (
        P("dp", "row", "col", None),
        P("dp", None, "row", "col", None),
        P("dp", ("row", "col"), None),
        P("dp", ("row", "col"), None),
        P("dp", None, ("row", "col")),
        P("dp"),
        P("dp"),
        P(),
    )
    return jax.shard_map(
        local, mesh=mesh, in_specs=placed, out_specs=P("dp", "row", "col", None), check_vma=False
    )
```

```python
import functools
import math

import jax
import jax.numpy as jnp
from jax import lax
from jax.experimental import pallas as pl
from jax.experimental.pallas import tpu as pltpu
from jax.sharding import PartitionSpec as P

HDIM = 128
RADIUS = 3
F32 = jnp.float32
BF16 = jnp.bfloat16
GROUP = 4
EDGE = 4
PAD_ROWS = 2


def attend_kernel(q_ref, kv_ref, up_ref, down_ref, far_ref, near_ref, out_ref):
    rows, cols = 12, 16
    inner = q_ref.shape[1]
    row0 = lax.axis_index("row") * rows
    col_index = lax.axis_index("col")
    col0 = col_index * cols
    core = lax.rem(col_index, 2)
    near_base = jnp.where(core == 0, cols, -EDGE)
    far_base = jnp.where(core == 0, -EDGE, cols)
    queries = GROUP * cols
    band = (GROUP + 2 * RADIUS) * cols
    side = (GROUP + 2 * RADIUS + PAD_ROWS) * EDGE
    keys = band + 2 * side
    halo = RADIUS * cols
    factor = math.log2(math.e) / math.sqrt(HDIM)
    q_id = lax.broadcasted_iota(jnp.int32, (queries, keys), 0)
    k_id = lax.broadcasted_iota(jnp.int32, (queries, keys), 1)
    q_row, q_col = q_id // cols, q_id % cols
    side_id = jnp.where(k_id < band + side, k_id - band, k_id - band - side)
    k_row = jnp.where(k_id < band, k_id // cols, side_id // EDGE)
    base = jnp.where(k_id < band + side, near_base, far_base)
    k_col = jnp.where(k_id < band, k_id % cols, base + side_id % EDGE)
    d_row, d_col = k_row - q_row, k_col - q_col
    reach = (d_row >= 0) & (d_row <= 2 * RADIUS) & (d_col >= -RADIUS) & (d_col <= RADIUS)
    k_gcol = col0 + k_col
    reach = reach & (k_gcol >= 0) & (k_gcol < cols * lax.axis_size("col"))
    ones = jnp.ones((keys, HDIM), BF16)
    for group in range(rows // GROUP):
        k_grow = row0 + GROUP * group - RADIUS + k_row
        allowed = reach & (k_grow >= 0) & (k_grow < rows * lax.axis_size("row"))
        bias = jnp.where(allowed, F32(0.0), F32(-1e30))
        first = (GROUP * group - RADIUS) * cols
        last = first + band
        for head in range(inner // HDIM):
            lanes = slice(head * HDIM, (head + 1) * HDIM)

            def gathered(which):
                parts = []
                if first < 0:
                    parts.append(up_ref[which, halo + first : halo, lanes])
                parts.append(kv_ref[which, max(first, 0) : min(last, rows * cols), lanes])
                if last > rows * cols:
                    parts.append(down_ref[which, 0 : last - rows * cols, lanes])
                span = slice(GROUP * group * EDGE, GROUP * group * EDGE + side)
                parts.append(near_ref[which, span, lanes])
                parts.append(far_ref[which, span, lanes])
                return jnp.concatenate(parts, axis=0)

            q = q_ref[group * queries : (group + 1) * queries, lanes]
            scores = lax.dot_general(
                q, gathered(0), (((1,), (1,)), ((), ())), preferred_element_type=F32
            )
            scores = scores + bias
            top = jnp.max(scores, axis=-1, keepdims=True)
            weight = jnp.exp2((scores - top) * factor).astype(BF16)
            values = jnp.concatenate([gathered(1), ones], axis=1)
            both = jnp.dot(weight, values, preferred_element_type=F32)
            out_ref[group * queries : (group + 1) * queries, lanes] = (
                both[:, :HDIM] / both[:, HDIM:]
            ).astype(BF16)


def attend(q, kv, up, down, far, near):
    tokens, inner = q.shape
    return pl.pallas_call(
        attend_kernel,
        out_shape=jax.ShapeDtypeStruct((tokens, inner), BF16),
        in_specs=[pl.BlockSpec(memory_space=pltpu.VMEM)] * 6,
        out_specs=pl.BlockSpec(memory_space=pltpu.VMEM),
        compiler_params=pltpu.CompilerParams(vmem_limit_bytes=20 * 2**20),
        cost_estimate=pl.CostEstimate(flops=3000000000, bytes_accessed=0, transcendentals=0),
        name="attend",
    )(q, kv, up, down, far, near)


def in_vmem(count):
    return [pl.BlockSpec(memory_space=pltpu.VMEM)] * count


def picked_row(label, table_ref):
    columns, count = table_ref.shape
    kept = jnp.zeros((columns, 128), F32)
    for first in range(0, count, 128):
        width = min(128, count - first)
        block = table_ref[:, first : first + width].astype(F32)
        if width < 128:
            block = jnp.concatenate([block, jnp.zeros((columns, 128 - width), F32)], axis=1)
        ids = lax.broadcasted_iota(jnp.int32, (columns, 128), 1) + first
        kept = kept + jnp.where(ids.astype(F32) == label, block, F32(0.0))
    ones = jnp.ones((16, 128), BF16)
    return lax.dot_general(ones, kept.astype(BF16), (((1,), (1,)), ((), ())), preferred_element_type=F32)


def gate_product(row_a, row_b, embed, gate_weight):
    value = (0.5 * (row_a + row_b)).astype(BF16).astype(F32) + embed
    cond = (value / (1.0 + jnp.exp(-value))).astype(BF16)
    part = jnp.dot(cond, gate_weight, preferred_element_type=F32)
    return jnp.concatenate([part[:1, at * 128 : (at + 1) * 128] for at in range(16)], axis=0)


def to_block(value):
    high = value.astype(BF16).astype(F32)
    return jnp.concatenate([high, value - high], axis=0).astype(BF16)


def from_block(block):
    block = block.astype(F32)
    return block[:16] + block[16:]


FETCHES = 4


def begin_kernel(label_ref, step_ref, table_ref, gate_ref, ask_ref, table_out, gate_out, numbers, sems):
    label_copy = pltpu.make_async_copy(label_ref, numbers.at[0], sems.at[2 * FETCHES])
    step_copy = pltpu.make_async_copy(step_ref, numbers.at[1], sems.at[2 * FETCHES + 1])
    label_copy.start()
    step_copy.start()
    copies = []
    for kind, (source, target) in enumerate(((table_ref, table_out), (gate_ref, gate_out))):
        rows = source.shape[0] // FETCHES
        for part in range(FETCHES):
            span = pl.ds(part * rows, rows)
            copies.append(
                pltpu.make_async_copy(source.at[span, :], target.at[span, :], sems.at[kind * FETCHES + part])
            )
            copies[-1].start()
    shard_width, half_width = gate_ref.shape[0], gate_ref.shape[1] // 2
    first = (lax.axis_index("row") * lax.axis_size("col") + lax.axis_index("col")) * shard_width
    positions = lax.broadcasted_iota(jnp.int32, (1, shard_width), 1) + first
    freq_index = jnp.where(positions < half_width, positions, positions - half_width).astype(F32)
    frequency = jnp.exp(-math.log(10000.0) * freq_index / half_width)
    label_copy.wait()
    step_copy.wait()
    angle = jnp.full((1, 1), numbers[1, 0], jnp.int32).astype(F32) * frequency
    embed = jnp.where(positions < half_width, jnp.cos(angle), jnp.sin(angle))
    label = jnp.full((1, 1), numbers[0, 0], jnp.int32).astype(F32)
    for copy in copies[:FETCHES]:
        copy.wait()
    row = picked_row(label, table_out)[:1]
    ask_ref[:, 0:128] = jnp.concatenate([row, embed], axis=1)
    ask_ref[:, 128:256] = jnp.broadcast_to(label, (1, 128))
    for copy in copies[FETCHES:]:
        copy.wait()


def begin(label, step, table, gate_weight):
    return pl.pallas_call(
        begin_kernel,
        out_shape=(
            jax.ShapeDtypeStruct((1, 256), F32),
            jax.ShapeDtypeStruct(table.shape, BF16),
            jax.ShapeDtypeStruct(gate_weight.shape, BF16),
        ),
        in_specs=[pl.BlockSpec(memory_space=pltpu.HBM)] * 4,
        out_specs=tuple(in_vmem(3)),
        scratch_shapes=[pltpu.SMEM((2, 1), jnp.int32), pltpu.SemaphoreType.DMA((2 * FETCHES + 2,))],
        compiler_params=pltpu.CompilerParams(vmem_limit_bytes=56 * 2**20),
        name="begin",
    )(label, step, table, gate_weight)


def answer_kernel(asked_ref, table_ref, gate_ref, answer_ref):
    row = picked_row(asked_ref[:, 128:129], table_ref)
    part = gate_product(row, asked_ref[:, 0:64], asked_ref[:, 64:128], gate_ref[...])
    answer_ref[:, 0:128] = to_block(part)
    rows = jnp.concatenate([row, row], axis=1)
    answer_ref[:, 128:256] = jnp.concatenate([rows, rows], axis=0).astype(BF16)


def answer(asked, table, gate_weight):
    return pl.pallas_call(
        answer_kernel,
        out_shape=jax.ShapeDtypeStruct((32, 256), BF16),
        in_specs=in_vmem(3),
        out_specs=pl.BlockSpec(memory_space=pltpu.VMEM),
        compiler_params=pltpu.CompilerParams(vmem_limit_bytes=8 * 2**20),
        cost_estimate=pl.CostEstimate(flops=5000000000, bytes_accessed=0, transcendentals=0),
        name="answer",
    )(asked, table, gate_weight)


def mix_kernel(own_ref, peer_ref, ask_ref, answered_ref, gate_ref, sent_ref):
    shard, width = own_ref.shape
    peer = peer_ref[...].astype(F32)
    sent_ref[:, 0:width] = (0.5 * (own_ref[...].astype(F32) + peer)).astype(BF16)
    own_row = jnp.broadcast_to(ask_ref[:, 0:64], (16, 64))
    peer_row = answered_ref[0:16, 128:192].astype(F32)
    part = gate_product(own_row, peer_row, ask_ref[:, 64:128], gate_ref[...])
    part = 0.5 * (part + from_block(answered_ref[:, 0:128]))
    sent_ref[:, width : width + 128] = to_block(part)


def mix(own, peer, ask, answered, gate_weight):
    shard, width = own.shape
    return pl.pallas_call(
        mix_kernel,
        out_shape=jax.ShapeDtypeStruct((shard, width + 128), BF16),
        in_specs=in_vmem(5),
        out_specs=pl.BlockSpec(memory_space=pltpu.VMEM),
        compiler_params=pltpu.CompilerParams(vmem_limit_bytes=8 * 2**20),
        cost_estimate=pl.CostEstimate(flops=5000000000, bytes_accessed=0, transcendentals=0),
        name="mix",
    )(own, peer, ask, answered, gate_weight)


def stack_kernel(*refs):
    parts, out_ref = [refs[at] for at in (0, 3, 1, 2)], refs[4]
    shard = parts[0].shape[0]
    for index, part in enumerate(parts):
        out_ref[index * shard : (index + 1) * shard, :] = part[...]


def stacked(parts):
    rows, width = parts[0].shape
    return pl.pallas_call(
        stack_kernel,
        out_shape=jax.ShapeDtypeStruct((4 * rows, width), BF16),
        in_specs=in_vmem(4),
        out_specs=pl.BlockSpec(memory_space=pltpu.VMEM),
        compiler_params=pltpu.CompilerParams(vmem_limit_bytes=8 * 2**20),
        cost_estimate=pl.CostEstimate(flops=5000000000, bytes_accessed=0, transcendentals=0),
        name="stack",
    )(*parts)


def cut_kernel(kv_ref, after_ref, low_ref, high_ref, sems):
    tokens, halo = kv_ref.shape[1], low_ref.shape[1]
    lower = pltpu.make_async_copy(kv_ref.at[:, pl.ds(tokens - halo, halo), :], low_ref, sems.at[0])
    upper = pltpu.make_async_copy(kv_ref.at[:, pl.ds(0, halo), :], high_ref, sems.at[1])
    lower.start()
    upper.start()
    lower.wait()
    upper.wait()


def cut(kv, after):
    edge = jax.ShapeDtypeStruct((2, RADIUS * 16, kv.shape[2]), BF16)
    return pl.pallas_call(
        cut_kernel,
        out_shape=(edge, edge),
        in_specs=[pl.BlockSpec(memory_space=pl.ANY)] * 2,
        out_specs=tuple(in_vmem(2)),
        scratch_shapes=[pltpu.SemaphoreType.DMA((2,))],
        compiler_params=pltpu.CompilerParams(vmem_limit_bytes=8 * 2**20),
        name="cut",
    )(kv, after)


def edges_kernel(kv_ref, up_ref, down_ref, after_ref, near_ref, far_ref):
    cols = 16
    core = lax.rem(lax.axis_index("col"), 2)
    count = near_ref.shape[1]
    source = up_ref.shape[1] + kv_ref.shape[1] + down_ref.shape[1]
    out_id = lax.broadcasted_iota(jnp.int32, (count, source), 0)
    in_id = lax.broadcasted_iota(jnp.int32, (count, source), 1)
    right = (out_id // EDGE) * cols + cols - EDGE + out_id % EDGE
    left = (out_id // EDGE) * cols + out_id % EDGE
    right = jnp.where(in_id == right, F32(1.0), F32(0.0))
    left = jnp.where(in_id == left, F32(1.0), F32(0.0))
    first = core == 0
    pick_near = jnp.where(first, right, left).astype(BF16)
    pick_far = jnp.where(first, left, right).astype(BF16)
    for which in range(2):
        tall = jnp.concatenate([up_ref[which], kv_ref[which], down_ref[which]], axis=0)
        near_ref[which] = jnp.dot(pick_near, tall, preferred_element_type=F32).astype(BF16)
        far_ref[which] = jnp.dot(pick_far, tall, preferred_element_type=F32).astype(BF16)


def edges(kv, up, down, after):
    inner = kv.shape[2]
    count = (12 + 2 * RADIUS + PAD_ROWS) * EDGE
    edge = jax.ShapeDtypeStruct((2, count, inner), BF16)
    return pl.pallas_call(
        edges_kernel,
        out_shape=(edge, edge),
        in_specs=in_vmem(3) + [pl.BlockSpec(memory_space=pl.ANY)],
        out_specs=tuple(in_vmem(2)),
        compiler_params=pltpu.CompilerParams(vmem_limit_bytes=12 * 2**20),
        name="edges",
    )(kv, up, down, after)


def weight_rows(even, odd, at):
    rows = []
    for back in range(4):
        span = slice(back * 32, (back + 1) * 32)
        rows += [even[span, at], odd[span, at]]
    return rows


def gate_sum(pieces, width):
    total = jnp.zeros((32, 128), F32)
    for piece in pieces:
        for back in range(4):
            total = total + piece[back * 32 : (back + 1) * 32, width : width + 128].astype(F32)
    return total


def begin_project_kernel(a_ref, own, other, beside, own_x, other_x, beside_x, sum_ref, lanes_ref, gate_ref, held_ref):
    row, col = lax.axis_index("row"), lax.axis_index("col")
    core, place = lax.rem(col, 2), lax.div(col, 2)
    block = 256
    width = sum_ref.shape[1]
    odd_place, high_place = place & 1, place >= 2
    for back in range(4):
        start = pl.multiple_of((row ^ back) * block, block)
        lanes = a_ref[:, pl.ds(start, block)].astype(F32)
        first, second = lanes[:, :128], lanes[:, 128:]
        halves = jnp.where(high_place, second, first), jnp.where(high_place, first, second)
        halves = [pltpu.roll(half, 64 * odd_place, 1).astype(BF16) for half in halves]
        for slot, step in enumerate((0, 1, 3)):
            at = (step % 2) * 64
            held_ref[:, slot * block + back * 64 : slot * block + (back + 1) * 64] = halves[step // 2][:, at : at + 64]
        lanes_ref[:, back * 64 : (back + 1) * 64] = halves[1][:, :64]
    gate_ref[...] = gate_sum((own, beside, other, own_x, beside_x, other_x), width)
    part_width = 512

    def multiply(even, odd):
        for part in range(width // part_width):
            at = slice(part * part_width, (part + 1) * part_width)
            rows = []
            for even_piece, odd_piece in zip(even, odd):
                rows += weight_rows(even_piece, odd_piece, at)
            sum_ref[:, at] = jnp.dot(held_ref[...], jnp.concatenate(rows, axis=0), preferred_element_type=F32)

    @pl.when(core == 0)
    def _():
        multiply((own, beside, other), (own_x, beside_x, other_x))

    @pl.when(core == 1)
    def _():
        multiply((own_x, beside_x, other_x), (own, beside, other))


def begin_project(a, pieces):
    tokens, inner = a.shape
    width = pieces[0].shape[1] - 128
    return pl.pallas_call(
        begin_project_kernel,
        out_shape=(
            jax.ShapeDtypeStruct((tokens, width), F32),
            jax.ShapeDtypeStruct((tokens, inner // 4), BF16),
            jax.ShapeDtypeStruct((32, 128), F32),
        ),
        in_specs=in_vmem(7),
        out_specs=tuple(in_vmem(3)),
        scratch_shapes=[pltpu.VMEM((tokens, inner - inner // 4), BF16)],
        compiler_params=pltpu.CompilerParams(vmem_limit_bytes=20 * 2**20),
        name="begin_project",
    )(a, *pieces)


def project_kernel(sum_ref, lanes_ref, gate_ref, piece, piece_x, out_ref):
    core = lax.rem(lax.axis_index("col"), 2)
    width = out_ref.shape[1]
    total = gate_ref[...] + gate_sum((piece, piece_x), width)
    total = total[:16] + total[16:]
    gate = jnp.concatenate([total[at : at + 1] for at in range(16)], axis=1)
    part_width = 512

    def multiply(even, odd):
        for part in range(width // part_width):
            at = slice(part * part_width, (part + 1) * part_width)
            rows = jnp.concatenate(weight_rows(even, odd, at), axis=0)
            product = jnp.dot(lanes_ref[...], rows, preferred_element_type=F32) + sum_ref[:, at]
            out_ref[:, at] = (gate[:, at] * product).astype(BF16)

    @pl.when(core == 0)
    def _():
        multiply(piece, piece_x)

    @pl.when(core == 1)
    def _():
        multiply(piece_x, piece)


def project(begun, piece, piece_x):
    tokens, width = begun[0].shape
    return pl.pallas_call(
        project_kernel,
        out_shape=jax.ShapeDtypeStruct((tokens, width), BF16),
        in_specs=in_vmem(5),
        out_specs=pl.BlockSpec(memory_space=pltpu.VMEM),
        compiler_params=pltpu.CompilerParams(vmem_limit_bytes=16 * 2**20),
        name="project",
    )(*begun, piece, piece_x)


def local(queries, keyvals, out_weight, gate_weight, class_table, labels, timesteps, round_index):
    dp_count, row_count, col_count = (lax.axis_size(a) for a in ("dp", "row", "col"))
    bit_count = dp_count.bit_length() - 1
    tile_rows, tile_cols, inner = queries.shape[1:]
    up_pairs = [(i, i + 1) for i in range(row_count - 1)]
    down_pairs = [(j, i) for i, j in up_pairs]
    near_pairs = [(i, i ^ 1) for i in range(col_count)]
    far_pairs = [(i, i + 1) for i in range(1, col_count - 1, 2)]
    far_pairs = far_pairs + [(j, i) for i, j in far_pairs]

    def body(distance, ask, table, gate_weight, out_weight, q, kv):
        ahead = [(i, (i + distance) % dp_count) for i in range(dp_count)]
        behind = [(j, i) for i, j in ahead]
        asked = lax.ppermute(ask, "dp", behind)
        peer = lax.ppermute(out_weight, "dp", ahead)
        low, high = cut(kv, ask)
        up = lax.ppermute(low, "row", up_pairs)
        down = lax.ppermute(high, "row", down_pairs)
        answered = lax.ppermute(answer(asked, table, gate_weight), "dp", ahead)
        sent = mix(out_weight, peer, ask, answered, gate_weight)
        got = [sent] + [
            lax.ppermute(sent, "row", [(i, i ^ k) for i in range(row_count)]) for k in (2, 3, 1)
        ]
        stack = stacked(got)
        opposite, beside, other = (
            lax.ppermute(stack, "col", [(i, i ^ (2 * k)) for i in range(col_count)]) for k in (2, 1, 3)
        )
        near, far = edges(kv, up, down, sent)
        far = lax.ppermute(far, "col", far_pairs)
        near = lax.ppermute(near, "col", near_pairs)
        attended = attend(q, kv, up, down, far, near)
        mine, attended = lax.optimization_barrier((stack, attended))
        siblings = [lax.ppermute(part, "col", near_pairs) for part in (mine, opposite, other, beside)]
        mine_x, opposite_x, other_x, beside_x = siblings
        begun = begin_project(attended, (stack, other, beside, mine_x, other_x, beside_x))
        return project(begun, opposite, opposite_x)

    table = class_table[0].T
    ask, table, gate_weight = begin(labels, timesteps, table, gate_weight[0])
    result = lax.switch(
        round_index[0] % bit_count,
        [functools.partial(body, 2**bit) for bit in range(bit_count)],
        ask,
        table,
        gate_weight,
        out_weight[0],
        queries.reshape(-1, inner),
        keyvals.reshape(2, -1, inner),
    )
    return result.reshape(1, tile_rows, tile_cols, -1)


def solution(mesh):
    placed = (
        P("dp", "row", "col", None),
        P("dp", None, "row", "col", None),
        P("dp", ("row", "col"), None),
        P("dp", ("row", "col"), None),
        P("dp", None, ("row", "col")),
        P("dp"),
        P("dp"),
        P(),
    )
    return jax.shard_map(
        local, mesh=mesh, in_specs=placed, out_specs=P("dp", "row", "col", None), check_vma=False
    )
```
